256 devices in a mesh: sec: 32 (over x, z), term: 8 (over y, core).
Axes of the slice: x: 4, y: 4, z: 8, core: 2. Of those that a mesh axis runs over, the one named last changes fastest.
Arguments:
- psi_blocks: float32 [256, 256, 256], P('sec'), may hold values from -6 to 6
- left_env: float32 [16, 256, 256, 256], P('term', 'sec'), may hold values from -0.1875 to 0.1875
- right_env: float32 [16, 256, 256, 256], P('term', 'sec'), may hold values from -0.75 to 0.75
- left_sizes: int32 [256], P('sec'), may hold values from 1 to 256, 16384 in all
- right_sizes: int32 [256], P('sec'), may hold values from 1 to 256, 16384 in all
- dest_sector: int32 [16, 256], P('term', 'sec'), may hold values from 0 to 255, as said below
Outputs:
- sigma_blocks: float32 [256, 256, 256], P('sec')
The draws below stay inside these ranges and needn't reach their ends.
Inputs may be any that keep to these rules, and one draw needn't show every extreme that they name: `left_sizes`: the entries sum to 16384, and the largest equals 256. `right_sizes`: the entries sum to 16384, and the largest equals 256. For every term t, dest_sector[t] is a permutation of the 256 sectors; sector s is held by index s // 8 of sec; of the 16 pairs (term, sector) held by one device, at most 1 reach sectors held by any one index of sec, and exactly 1 reach some index.
All inputs are finite; a program needn't handle non-finite values. No bound on the sum of `left_sizes` or of `right_sizes` on one device may be relied on, other than what follows from the above.
Results may differ from the reference program's by a relative error of at most 0.0001.
Values sent between devices are 32-bit elements; how exact they have to be, the bound alone decides.
No kernel may reach another device: no remote copies, remote signals or barrier semaphores. Data moves between devices by JAX's collectives and lax.ppermute only.
A program may use at most 128 MiB of HBM per device.

```python
import math
import jax
import jax.numpy as jnp
import numpy as np
from jax import lax

BLK = 256
SEC_DEV = 8
TERM_DEV = 2
NSEC = 256
TERMS = 16


def draw_dest_sector(key, part):
    key = jax.random.fold_in(key, 7)
    device_count = NSEC // SEC_DEV
    member_count = TERMS // TERM_DEV
    capacity = (TERM_DEV * SEC_DEV + device_count - 1) // device_count
    key_outer, key_inner, key_offset, key_place = jax.random.split(key, 4)
    outer_perm = jax.random.permutation(key_outer, device_count)
    inner_perm = jax.random.permutation(key_inner, device_count)
    offsets = jax.vmap(lambda single: jax.random.permutation(single, device_count))(jax.random.split(key_offset, member_count))
    places = jax.vmap(lambda single: jax.random.permutation(single, SEC_DEV))(jax.random.split(key_place, TERMS))
    term_index = jnp.arange(TERMS, dtype=jnp.int32)[:, None]
    sector_index = jnp.arange(NSEC, dtype=jnp.int32)[None, :]
    source_device = sector_index // SEC_DEV
    within_device = sector_index % SEC_DEV
    member_index = term_index // TERM_DEV
    local_term = term_index % TERM_DEV
    group_index = (local_term * SEC_DEV + within_device) // capacity
    shifted = offsets[member_index, group_index]
    target_device = outer_perm[(inner_perm[source_device] + shifted) % device_count]
    target_place = places[term_index, within_device]
    return (target_device * SEC_DEV + target_place).astype(jnp.int32)


def steps_of(own_key, extent, cuts, smallest, high):
    factor_of, own = 1.0, jax.random.fold_in(own_key, 6)
    for axis_at, shards_of in cuts:
        draws = jnp.exp(jax.random.uniform(jax.random.fold_in(own, axis_at), (shards_of,), jnp.float32, smallest / len(cuts), high / len(cuts)))
        factor_of = factor_of * jnp.repeat(draws, extent[axis_at] // shards_of).reshape([-1 if axis == axis_at else 1 for axis in range(len(extent))])
    return factor_of


def length_profile(count, total, reach, skew):
    weights = [(1 << 20) // math.isqrt(rank ** skew) + 1 for rank in range(2, count + 1)]
    surplus, holding = total - reach - (count - 1), [1] * (count - 1)
    while surplus > 0:
        free = [i for i in range(count - 1) if holding[i] < reach]
        pool, left = sum([weights[i] for i in free]), surplus
        for i in free:
            extra = min(reach - holding[i], max(1, left * weights[i] // pool), surplus)
            holding[i] = holding[i] + extra
            surplus = surplus - extra
    return np.array([reach] + holding)


def ragged(stream_key, number_of, total, limit, slope):
    if number_of == 2:
        one = jax.random.randint(stream_key, (), max(1, total - limit), min(limit, total - 1) + 1)
        return jnp.stack([one, total - one])
    lengths = jnp.asarray(length_profile(number_of, total, limit, slope), jnp.int32)
    pairs = (number_of - 1) // 2
    source_of, taker = lengths[1:1 + 2 * pairs:2], lengths[2:2 + 2 * pairs:2]
    slack = jnp.minimum(source_of - 1, limit - taker)
    passed = jax.random.randint(jax.random.fold_in(stream_key, 1), (pairs,), 0, 1 << 20) % (slack + 1)
    lengths = lengths.at[1:1 + 2 * pairs:2].set(source_of - passed).at[2:2 + 2 * pairs:2].set(taker + passed)
    return lengths[jax.random.permutation(jax.random.fold_in(stream_key, 2), number_of)]


def bell_draw(own_key, shape, width, limit, shards=(), kind=jnp.bfloat16):
    entries = jax.random.normal(own_key, shape, jnp.float32) * width
    if len(shards) > 0:
        entries = steps_of(own_key, shape, shards, -0.22, 0.18) * entries
    return jnp.clip(entries, min=-limit, max=limit).astype(kind)


def setup_inputs(seed: int = 0) -> dict:
    key_of = jax.random.split(jax.random.key(seed), 7)
    return {
        "psi_blocks": bell_draw(key_of[0], (NSEC, BLK, BLK), 1.0, 6.0, ((0, 32),), jnp.float32),
        "left_env": bell_draw(key_of[1], (TERMS, NSEC, BLK, BLK), (BLK * TERMS // 4) ** -0.5, 0.1875, ((0, 8), (1, 32)), jnp.float32),
        "right_env": bell_draw(key_of[2], (TERMS, NSEC, BLK, BLK), (BLK // 4) ** -0.5, 0.75, ((0, 8), (1, 32)), jnp.float32),
        "left_sizes": ragged(key_of[3], NSEC, BLK * NSEC // 4, BLK, 2).astype(jnp.int32),
        "right_sizes": ragged(key_of[4], NSEC, BLK * NSEC // 4, BLK, 2).astype(jnp.int32),
        "dest_sector": draw_dest_sector(jax.random.fold_in(key_of[6], 71), 0),
    }


def sector_mask(left_sizes, right_sizes, block_size):
    positions = jnp.arange(block_size, dtype=jnp.int32)
    row_ok = positions[None, :, None] < left_sizes[:, None, None]
    col_ok = positions[None, None, :] < right_sizes[:, None, None]
    return (row_ok & col_ok).astype(jnp.float32)


def reference(psi_blocks, left_env, right_env, left_sizes, right_sizes, dest_sector):
    block_size = psi_blocks.shape[1]
    valid_mask = sector_mask(left_sizes, right_sizes, block_size)
    masked_psi = psi_blocks * valid_mask

    def one_term(sigma_acc, inputs):
        left_term, right_term, targets = inputs
        carried = jnp.einsum('sab,sbc->sac', masked_psi, right_term, precision=lax.Precision.HIGHEST)
        landed = jnp.einsum('sab,sbc->sac', left_term[targets], carried, precision=lax.Precision.HIGHEST)
        return sigma_acc.at[targets].add(landed), None

    start_acc = jnp.zeros(psi_blocks.shape, jnp.float32)
    sigma_acc, unused_out = lax.scan(one_term, start_acc, (left_env, right_env, dest_sector))
    return sigma_acc * valid_mask
```

```python
import functools
import jax
import jax.numpy as jnp
from jax import lax
from jax.experimental import pallas as pl
from jax.experimental.pallas import tpu as pltpu
from jax.sharding import PartitionSpec as P

BLK = 256
LANES = 128
ROWS = 8
PEERS = 32
MEMBERS = 8
HELD = 8
PAIRS = 16
ROWS_OUT = 64
ROWS_IN = 64
PIECE = 32
VMEM_BYTES = 40 * 1024 * 1024


def sector_mask(left_sizes, right_sizes, block_size):
    positions = jnp.arange(block_size, dtype=jnp.int32)
    row_ok = positions[None, :, None] < left_sizes[:, None, None]
    col_ok = positions[None, None, :] < right_sizes[:, None, None]
    return (row_ok & col_ok).astype(jnp.float32)


def pack_blocks(outgoing, targets, term_ids, sector_local, capacity, slot_count):
    target_device = targets // sector_local
    target_place = targets % sector_local
    count_out = targets.shape[0]
    order_index = jnp.arange(count_out, dtype=jnp.int32)
    same_device = target_device[:, None] == target_device[None, :]
    earlier = order_index[None, :] < order_index[:, None]
    peer_rank = jnp.sum((same_device & earlier).astype(jnp.int32), axis=1)
    send_slot = target_device * capacity + peer_rank
    chosen = jnp.arange(slot_count, dtype=jnp.int32)[:, None] == send_slot[None, :]
    slot_source = jnp.sum(jnp.where(chosen, order_index[None, :], 0), axis=1)
    filled = jnp.any(chosen, axis=1)
    buffer = jnp.where(filled[:, None, None], outgoing[slot_source], 0.0)
    left_code = term_ids * sector_local + target_place
    meta_codes = jnp.where(filled, left_code[slot_source], -1)
    return (buffer, meta_codes)


def apply_left(received, meta_codes, flat_left, sector_local, live_count):
    slot_count = meta_codes.shape[0]
    is_valid = meta_codes >= 0
    live_rank = jnp.cumsum(is_valid.astype(jnp.int32)) - 1
    wanted = jnp.arange(live_count, dtype=jnp.int32)
    picked = (live_rank[None, :] == wanted[:, None]) & is_valid[None, :]
    slot_index = jnp.arange(slot_count, dtype=jnp.int32)
    source_slot = jnp.sum(jnp.where(picked, slot_index[None, :], 0), axis=1)
    compact_blocks = received[source_slot]
    compact_codes = meta_codes[source_slot]
    chosen_left = flat_left[compact_codes]
    landed = jnp.einsum(
        "pab,pbc->pac", chosen_left, compact_blocks, precision=lax.Precision.HIGHEST
    )
    target_place = compact_codes % sector_local
    onehot_place = target_place[:, None] == jnp.arange(sector_local, dtype=jnp.int32)[None, :]
    return jnp.einsum(
        "pk,pac->kac", onehot_place.astype(jnp.float32), landed, precision=lax.Precision.HIGHEST
    )


def dense_program(psi_blocks, left_env, right_env, left_sizes, right_sizes, dest_sector):
    term_local = left_env.shape[0]
    sector_local = left_env.shape[1]
    block_size = left_env.shape[2]
    peers = lax.axis_size("sec")
    capacity = (term_local * sector_local + peers - 1) // peers
    slot_count = peers * capacity
    valid_mask = sector_mask(left_sizes, right_sizes, block_size)
    masked_psi = psi_blocks * valid_mask
    carried = jnp.einsum("sab,tsbc->tsac", masked_psi, right_env, precision=lax.Precision.HIGHEST)
    flat_left = left_env.reshape(term_local * sector_local, block_size, block_size)
    term_ids = jnp.repeat(jnp.arange(term_local, dtype=jnp.int32), sector_local)
    buffer, meta_codes = pack_blocks(
        carried.reshape(term_local * sector_local, block_size, block_size),
        dest_sector.reshape(term_local * sector_local),
        term_ids,
        sector_local,
        capacity,
        slot_count,
    )
    received, codes_in = (
        lax.all_to_all(buffer, "sec", split_axis=0, concat_axis=0, tiled=True),
        lax.all_to_all(meta_codes, "sec", split_axis=0, concat_axis=0, tiled=True),
    )
    partial_sum = apply_left(received, codes_in, flat_left, sector_local, term_local * sector_local)
    total = lax.psum(partial_sum, "term")
    return total * valid_mask


def split3(a):
    hi = a.astype(jnp.bfloat16)
    lo = (a - hi.astype(jnp.float32)).astype(jnp.bfloat16)
    return hi, lo


def dot3(a, b, transposed=False):
    dims = (((1,), (1 if transposed else 0,)), ((), ()))
    a_hi, a_lo = split3(a)
    b_hi, b_lo = split3(b)
    mul = functools.partial(
        lax.dot_general, dimension_numbers=dims, preferred_element_type=jnp.float32
    )
    return mul(a_hi, b_hi) + (mul(a_hi, b_lo) + mul(a_lo, b_hi))


T_START, T_ROWS, T_NX, T_NY, T_LEFT, T_RIGHT, T_BASE = 0, 1, 2, 3, 4, 5, 6
T_WIDTH = 10


def tile_rows(stream, rows):
    return (stream % 4) * (ROWS * rows) + stream // 4


def send_kernel(tbl, psi_ref, right_ref, buf_ref, x_ref, y_ref):
    row = lax.broadcasted_iota(jnp.int32, (BLK, BLK), 0)
    col = lax.broadcasted_iota(jnp.int32, (BLK, BLK), 1)

    def emit(src_ref, strip, first, rows):
        room = jnp.maximum(jnp.minimum(rows, 4 * ROWS_OUT - first), 0)

        def one(a, carry):
            tile = src_ref[pl.ds(pl.multiple_of(a * ROWS, ROWS), ROWS), pl.ds(strip * LANES, LANES)]
            buf_ref[pl.ds(tile_rows(first + a, ROWS_OUT), ROWS, stride=ROWS_OUT), :] = tile
            return carry

        lax.fori_loop(0, room, one, 0)

    def pair(p, carry):
        at = p * T_WIDTH
        start, rows = tbl[at + T_START], tbl[at + T_ROWS]
        nx, ny = tbl[at + T_NX], tbl[at + T_NY]
        kept = (row < tbl[at + T_LEFT]) & (col < tbl[at + T_RIGHT])
        psi = jnp.where(kept, psi_ref[p % HELD], 0.0)
        factors = (nx > 0) & (ny > 0)

        @pl.when(factors)
        def _():
            x_ref[...] = psi.T
            y_ref[...] = right_ref[p]

        @pl.when(nx == 0)
        def _():
            y_ref[...] = dot3(psi, right_ref[p])

        @pl.when(ny == 0)
        def _():
            x_ref[...] = dot3(psi, right_ref[p]).T

        for strip in range(2):
            @pl.when(strip < nx)
            def _():
                emit(x_ref, strip, start + strip * rows, rows)

        for strip in range(2):
            @pl.when(strip < ny)
            def _():
                emit(y_ref, strip, start + (nx + strip) * rows, rows)

        return carry

    lax.fori_loop(0, PAIRS, pair, 0)


def relay_kernel(idx, count, in_ref, out_ref):
    def slot(peer, carry):
        def some(i, inner):
            at = peer * ROWS_IN + i * ROWS
            for k in range(ROWS):
                out_ref[pl.ds(at + k, 1), :] = in_ref[pl.ds(idx[at + k], 1), :]
            return inner

        lax.fori_loop(0, (count[peer] + ROWS - 1) // ROWS, some, 0)
        return carry

    lax.fori_loop(0, PEERS, slot, 0)


def land_kernel(tbl, out_tbl, buf_ref, left_ref, keep_ref, send_ref, x_ref, y_ref, z_ref, acc_ref):
    acc_ref[...] = jnp.zeros_like(acc_ref)

    def take(dst_ref, strip, at, before, rows):
        start = tbl[at + T_START]

        def one(a, carry):
            q = before + a
            kind = (start + q) % 4
            rank = jnp.minimum(tbl[at + T_BASE + kind] + q // 4, ROWS_IN - 1)
            tile = buf_ref[pl.ds(kind * (ROWS * ROWS_IN) + rank, ROWS, stride=ROWS_IN), :]
            dst_ref[pl.ds(pl.multiple_of(a * ROWS, ROWS), ROWS), pl.ds(strip * LANES, LANES)] = tile
            return carry

        lax.fori_loop(0, rows, one, 0)

    def pair(u, carry):
        at = u * T_WIDTH
        rows, nx, ny = tbl[at + T_ROWS], tbl[at + T_NX], tbl[at + T_NY]

        @pl.when(nx > 0)
        def _():
            x_ref[...] = jnp.zeros_like(x_ref)
            for strip in range(2):
                @pl.when(strip < nx)
                def _():
                    take(x_ref, strip, at, strip * rows, rows)
            z_ref[...] = dot3(left_ref[u], x_ref[...], transposed=True)

        @pl.when(nx == 0)
        def _():
            z_ref[...] = left_ref[u]

        @pl.when(ny > 0)
        def _():
            y_ref[...] = jnp.zeros_like(y_ref)
            for strip in range(2):
                @pl.when(strip < ny)
                def _():
                    take(y_ref, strip, at, (nx + strip) * rows, rows)
            acc_ref[u % HELD] += dot3(z_ref[...], y_ref[...])

        @pl.when(ny == 0)
        def _():
            acc_ref[u % HELD] += z_ref[...]

        return carry

    lax.fori_loop(0, PAIRS, pair, 0)

    half = 4 * PIECE
    core, chip = out_tbl[O_CORE], out_tbl[O_CHIP]

    def sector(d, carry):
        first, rows, strips = out_tbl[3 * d], out_tbl[3 * d + 1], out_tbl[3 * d + 2]
        for strip in range(2):
            @pl.when(strip < strips)
            def _():
                begin = first + strip * rows
                room = jnp.maximum(jnp.minimum(rows, 2 * half - 1 - begin), 0)

                def one(a, inner):
                    s = begin + a
                    place = ((s % half) // PIECE ^ chip) * PIECE + s % PIECE
                    tile = acc_ref[
                        d,
                        pl.ds(pl.multiple_of(a * ROWS, ROWS), ROWS),
                        pl.ds(strip * LANES, LANES),
                    ]

                    @pl.when(s // half == core)
                    def _():
                        keep_ref[place] = tile

                    @pl.when(s // half != core)
                    def _():
                        send_ref[place] = tile

                    return inner

                lax.fori_loop(0, room, one, 0)
        return carry

    lax.fori_loop(0, HELD, sector, 0)
    flag = jnp.full((ROWS, LANES), out_tbl[O_FLAG], jnp.int32).astype(jnp.float32)
    last = (3 ^ chip) * PIECE + PIECE - 1

    @pl.when(core == 1)
    def _():
        keep_ref[last] = flag

    @pl.when(core != 1)
    def _():
        send_ref[last] = flag


def spread_kernel(out_tbl, sizes, own_ref, other_ref, out_ref):
    out_ref[...] = jnp.zeros_like(out_ref)
    half = 4 * PIECE
    core, chip = out_tbl[O_CORE], out_tbl[O_CHIP]
    row = lax.broadcasted_iota(jnp.int32, (ROWS, LANES), 0)
    col = lax.broadcasted_iota(jnp.int32, (ROWS, LANES), 1)

    def sector(d, carry):
        first, rows, strips = out_tbl[3 * d], out_tbl[3 * d + 1], out_tbl[3 * d + 2]
        height, width = sizes[d], sizes[HELD + d]
        for strip in range(2):
            @pl.when(strip < strips)
            def _():
                begin = first + strip * rows
                col_ok = col + strip * LANES < width

                def one(a, inner):
                    s = begin + a
                    place = ((s % half) // PIECE ^ chip) * PIECE + s % PIECE
                    kept = col_ok & (row + a * ROWS < height)
                    at = (
                        d,
                        pl.ds(pl.multiple_of(a * ROWS, ROWS), ROWS),
                        pl.ds(strip * LANES, LANES),
                    )

                    @pl.when(s // half == core)
                    def _():
                        out_ref[at] = jnp.where(kept, own_ref[place], 0.0)

                    @pl.when(s // half != core)
                    def _():
                        out_ref[at] = jnp.where(kept, other_ref[place], 0.0)

                    return inner

                lax.fori_loop(0, rows, one, 0)
        return carry

    lax.fori_loop(0, HELD, sector, 0)


O_CORE, O_CHIP, O_FLAG = 3 * HELD, 3 * HELD + 1, 3 * HELD + 2

SMEM = pl.BlockSpec(memory_space=pltpu.SMEM)
VMEM = pl.BlockSpec(memory_space=pltpu.VMEM)
PARAMS = pltpu.CompilerParams(vmem_limit_bytes=VMEM_BYTES)


def floats(*shape):
    return jax.ShapeDtypeStruct(shape, jnp.float32)


def scratch(*shape):
    return pltpu.VMEM(shape, jnp.float32)


def send_call(tbl, psi, right):
    return pl.pallas_call(
        send_kernel,
        out_shape=floats(PEERS * ROWS_OUT, LANES),
        in_specs=[SMEM, VMEM, VMEM],
        out_specs=VMEM,
        scratch_shapes=[scratch(BLK, BLK), scratch(BLK, BLK)],
        compiler_params=PARAMS,
    )(tbl, psi, right)


def relay_call(idx, count, received):
    return pl.pallas_call(
        relay_kernel,
        out_shape=floats(PEERS * ROWS_IN, LANES),
        in_specs=[SMEM, SMEM, VMEM],
        out_specs=VMEM,
        compiler_params=PARAMS,
    )(idx, count, received)


def land_call(tbl, out_tbl, received, left):
    return pl.pallas_call(
        land_kernel,
        out_shape=[floats(4 * PIECE, ROWS, LANES)] * 2,
        in_specs=[SMEM, SMEM, VMEM, VMEM],
        out_specs=[VMEM, VMEM],
        scratch_shapes=[scratch(BLK, BLK)] * 3 + [scratch(HELD, BLK, BLK)],
        compiler_params=PARAMS,
    )(tbl, out_tbl, received, left)


def spread_call(out_tbl, sizes, own, other):
    return pl.pallas_call(
        spread_kernel,
        out_shape=floats(HELD, BLK, BLK),
        in_specs=[SMEM, SMEM, VMEM, VMEM],
        out_specs=VMEM,
        compiler_params=PARAMS,
    )(out_tbl, sizes, own, other)


def up(value, unit):
    return (value + (unit - 1)) // unit


def before(values, axis):
    n = values.shape[axis]
    moved = jnp.moveaxis(values, axis, -1)
    lower = jnp.arange(n)[:, None] > jnp.arange(n)[None, :]
    total = jnp.sum(jnp.where(lower, moved[..., None, :], 0), axis=-1)
    return jnp.moveaxis(total, -1, axis)


def per_device(psi_blocks, left_env, right_env, left_sizes, right_sizes, dest_sector):
    me = lax.axis_index("sec")
    member = lax.axis_index("term")
    core, chip = member % 2, member // 2
    mine = jnp.concatenate([left_sizes, right_sizes, dest_sector.reshape(PAIRS)])
    facts = lax.all_to_all(
        jnp.broadcast_to(mine[None, :], (PEERS, 4 * HELD)), "sec", 0, 0, tiled=True
    )
    size_l, size_r, dest = facts[:, :HELD], facts[:, HELD : 2 * HELD], facts[:, 2 * HELD :]

    ls = jnp.concatenate([size_l, size_l], axis=1)
    rs = jnp.concatenate([size_r, size_r], axis=1)
    to_dev, to_place = dest // HELD, dest % HELD
    hit_dev = to_dev[:, :, None] == jnp.arange(PEERS)[None, None, :]
    hit_place = to_place[:, :, None] == jnp.arange(HELD)[None, None, :]
    rd = jnp.sum(
        jnp.where(hit_dev[:, :, :, None] & hit_place[:, :, None, :], size_r[None, None], 0),
        axis=(2, 3),
    )
    nl, nr = up(ls, LANES), up(rd, LANES)
    cost_c = up(ls, ROWS) * nr
    cost_ct = up(rd, ROWS) * nl
    cost_f = up(rs, ROWS) * (nl + nr)
    is_f = (cost_f < cost_c) & (cost_f < cost_ct)
    is_ct = ~is_f & (cost_ct < cost_c)
    rows = up(jnp.where(is_f, rs, jnp.where(is_ct, rd, ls)), ROWS)
    nx = jnp.where(is_f | is_ct, nl, 0)
    ny = jnp.where(is_ct, 0, nr)
    tiles = rows * (nx + ny)
    start = before(tiles, 1)
    total = jnp.sum(tiles, axis=1)

    kinds = jnp.arange(4)[:, None, None]
    lag = (kinds - start) % 4
    share = (tiles + 3 - lag) // 4
    first_row = (start + lag) // 4
    onto = jnp.sum(jnp.where(hit_dev[None], share[..., None], 0), axis=2)
    base = before(onto, 1)
    filled = jnp.sum(onto, axis=1)

    out_rows, out_strips = up(size_l, ROWS), up(size_r, LANES)
    out_tiles = out_rows * out_strips
    out_first = before(out_tiles, 1)
    spilled = (
        jnp.any(total > 4 * ROWS_OUT)
        | jnp.any(filled > ROWS_IN)
        | jnp.any(jnp.sum(out_tiles, axis=1) > MEMBERS * PIECE - 1)
    )

    def own(values, axis=0):
        return lax.dynamic_index_in_dim(values, me, axis, keepdims=False)

    zero = jnp.zeros((PAIRS,), jnp.int32)
    send_tbl = jnp.stack(
        [own(start), own(rows), own(nx), own(ny), own(ls), own(rs)] + [zero] * 4, axis=1
    ).reshape(-1)

    kind = me // ROWS
    onto_k = lax.dynamic_index_in_dim(onto, kind, 0, keepdims=False)
    base_k = lax.dynamic_index_in_dim(base, kind, 0, keepdims=False)
    first_k = lax.dynamic_index_in_dim(first_row, kind, 0, keepdims=False)
    filled_k = lax.dynamic_index_in_dim(filled, kind, 0, keepdims=False)
    first_to = jnp.sum(jnp.where(hit_dev, first_k[:, :, None], 0), axis=1)
    rank = jnp.arange(ROWS_IN)[None, None, :]
    here = (rank >= base_k[:, :, None]) & (rank < (base_k + onto_k)[:, :, None])
    origin = jnp.arange(PEERS)[:, None] * ROWS_OUT + first_to - base_k
    relay_idx = jnp.sum(jnp.where(here, origin[:, :, None] + rank, 0), axis=0)
    relay_idx = jnp.clip(relay_idx, 0, PEERS * ROWS_OUT - 1).reshape(-1)
    relay_count = jnp.minimum(filled_k, ROWS_IN)

    unit = jnp.arange(PAIRS)[:, None, None]
    reach = (dest[None] == me * HELD + unit % HELD) & (
        (jnp.arange(PAIRS) // HELD)[None, None, :] == unit // HELD
    )

    def reached(values):
        return jnp.sum(jnp.where(reach, values[None], 0), axis=(1, 2))

    base_me = lax.dynamic_index_in_dim(base, me, 2, keepdims=False)
    land_tbl = jnp.stack(
        [reached(start), reached(rows), reached(nx), reached(ny), reached(ls), reached(rs)]
        + [reached(jnp.broadcast_to(base_me[g][:, None], (PEERS, PAIRS))) for g in range(4)],
        axis=1,
    ).reshape(-1)

    out_tbl = jnp.concatenate(
        [
            jnp.stack([own(out_first), own(out_rows), own(out_strips)], axis=1).reshape(-1),
            jnp.stack([core, chip, spilled.astype(jnp.int32)]).astype(jnp.int32),
        ]
    )
    sizes = jnp.concatenate([left_sizes, right_sizes])

    sent = send_call(send_tbl, psi_blocks, right_env.reshape(PAIRS, BLK, BLK))
    hop = lax.all_to_all(sent.reshape(PEERS, ROWS_OUT, LANES), "sec", 0, 0, tiled=True)
    passed = relay_call(relay_idx, relay_count, hop.reshape(PEERS * ROWS_OUT, LANES))
    hop = lax.all_to_all(passed.reshape(PEERS, ROWS_IN, LANES), "sec", 0, 0, tiled=True)
    keep, give = land_call(
        land_tbl,
        out_tbl,
        hop.reshape(PEERS * ROWS_IN, LANES),
        left_env.reshape(PAIRS, BLK, BLK),
    )

    def swap(values, bits):
        return lax.ppermute(values, "term", [(i, i ^ bits) for i in range(MEMBERS)])

    half = (keep + swap(give, 1)).reshape(4, PIECE, ROWS, LANES)
    piece = half[0] + swap(half[1], 2) + swap(half[2], 4) + swap(half[3], 6)
    whole = jnp.concatenate([piece, swap(piece, 2), swap(piece, 4), swap(piece, 6)])
    other = swap(whole, 1)

    last = (3 ^ chip) * PIECE + PIECE - 1
    flag_own = lax.dynamic_slice(whole, (last, 0, 0), (1, 1, 1))
    flag_other = lax.dynamic_slice(other, (last, 0, 0), (1, 1, 1))
    flag = jnp.where(core == 1, flag_own, flag_other).reshape(())
    return lax.cond(
        flag > 0.5,
        lambda: dense_program(
            psi_blocks, left_env, right_env, left_sizes, right_sizes, dest_sector
        ),
        lambda: spread_call(out_tbl, sizes, whole, other),
    )


def solution(mesh):
    in_specs = (
        P("sec", None, None),
        P("term", "sec", None, None),
        P("term", "sec", None, None),
        P("sec"),
        P("sec"),
        P("term", "sec"),
    )
    out_specs = P("sec", None, None)
    return jax.shard_map(
        per_device, mesh=mesh, in_specs=in_specs, out_specs=out_specs, check_vma=False
    )
```

```python
import functools
import jax
import jax.numpy as jnp
from jax import lax
from jax.experimental import pallas as pl
from jax.experimental.pallas import tpu as pltpu
from jax.sharding import PartitionSpec as P

BLK = 256
LANES = 128
ROWS = 8
PEERS = 32
MEMBERS = 8
HELD = 8
PAIRS = 16
ROWS_OUT = 64
ROWS_IN = 64
PIECE = 32
VMEM_BYTES = 24 * 1024 * 1024
WIDE_BYTES = 56 * 1024 * 1024


def sector_mask(left_sizes, right_sizes, block_size):
    positions = jnp.arange(block_size, dtype=jnp.int32)
    row_ok = positions[None, :, None] < left_sizes[:, None, None]
    col_ok = positions[None, None, :] < right_sizes[:, None, None]
    return (row_ok & col_ok).astype(jnp.float32)


def pack_blocks(outgoing, targets, term_ids, sector_local, capacity, slot_count):
    target_device = targets // sector_local
    target_place = targets % sector_local
    count_out = targets.shape[0]
    order_index = jnp.arange(count_out, dtype=jnp.int32)
    same_device = target_device[:, None] == target_device[None, :]
    earlier = order_index[None, :] < order_index[:, None]
    peer_rank = jnp.sum((same_device & earlier).astype(jnp.int32), axis=1)
    send_slot = target_device * capacity + peer_rank
    chosen = jnp.arange(slot_count, dtype=jnp.int32)[:, None] == send_slot[None, :]
    slot_source = jnp.sum(jnp.where(chosen, order_index[None, :], 0), axis=1)
    filled = jnp.any(chosen, axis=1)
    buffer = jnp.where(filled[:, None, None], outgoing[slot_source], 0.0)
    left_code = term_ids * sector_local + target_place
    meta_codes = jnp.where(filled, left_code[slot_source], -1)
    return (buffer, meta_codes)


def apply_left(received, meta_codes, flat_left, sector_local, live_count):
    slot_count = meta_codes.shape[0]
    is_valid = meta_codes >= 0
    live_rank = jnp.cumsum(is_valid.astype(jnp.int32)) - 1
    wanted = jnp.arange(live_count, dtype=jnp.int32)
    picked = (live_rank[None, :] == wanted[:, None]) & is_valid[None, :]
    slot_index = jnp.arange(slot_count, dtype=jnp.int32)
    source_slot = jnp.sum(jnp.where(picked, slot_index[None, :], 0), axis=1)
    compact_blocks = received[source_slot]
    compact_codes = meta_codes[source_slot]
    chosen_left = flat_left[compact_codes]
    landed = jnp.einsum(
        "pab,pbc->pac", chosen_left, compact_blocks, precision=lax.Precision.HIGHEST
    )
    target_place = compact_codes % sector_local
    onehot_place = target_place[:, None] == jnp.arange(sector_local, dtype=jnp.int32)[None, :]
    return jnp.einsum(
        "pk,pac->kac", onehot_place.astype(jnp.float32), landed, precision=lax.Precision.HIGHEST
    )


def dense_program(psi_blocks, left_env, right_env, left_sizes, right_sizes, dest_sector):
    term_local = left_env.shape[0]
    sector_local = left_env.shape[1]
    block_size = left_env.shape[2]
    peers = lax.axis_size("sec")
    capacity = (term_local * sector_local + peers - 1) // peers
    slot_count = peers * capacity
    valid_mask = sector_mask(left_sizes, right_sizes, block_size)
    masked_psi = psi_blocks * valid_mask
    carried = jnp.einsum("sab,tsbc->tsac", masked_psi, right_env, precision=lax.Precision.HIGHEST)
    flat_left = left_env.reshape(term_local * sector_local, block_size, block_size)
    term_ids = jnp.repeat(jnp.arange(term_local, dtype=jnp.int32), sector_local)
    buffer, meta_codes = pack_blocks(
        carried.reshape(term_local * sector_local, block_size, block_size),
        dest_sector.reshape(term_local * sector_local),
        term_ids,
        sector_local,
        capacity,
        slot_count,
    )
    received, codes_in = (
        lax.all_to_all(buffer, "sec", split_axis=0, concat_axis=0, tiled=True),
        lax.all_to_all(meta_codes, "sec", split_axis=0, concat_axis=0, tiled=True),
    )
    partial_sum = apply_left(received, codes_in, flat_left, sector_local, term_local * sector_local)
    total = lax.psum(partial_sum, "term")
    return total * valid_mask


def split3(a):
    hi = a.astype(jnp.bfloat16)
    lo = (a - hi.astype(jnp.float32)).astype(jnp.bfloat16)
    return hi, lo


def dot3(a, b, transposed=False):
    dims = (((1,), (1 if transposed else 0,)), ((), ()))
    mul = functools.partial(
        lax.dot_general, dimension_numbers=dims, preferred_element_type=jnp.float32
    )
    return mul(a[0], b[0]) + (mul(a[0], b[1]) + mul(a[1], b[0]))


T_START, T_ROWS, T_NX, T_NY, T_LEFT, T_RIGHT, T_BASE = 0, 1, 2, 3, 4, 5, 6
T_WIDTH = 10


def tile_rows(stream, rows):
    return (stream % 4) * (ROWS * rows) + jnp.minimum(stream // 4, rows - 1)


def tile_at(a):
    return pl.ds(pl.multiple_of(a * ROWS, ROWS), ROWS)


def strip_at(strip):
    return pl.ds(strip * LANES, LANES)


def block_at(i):
    return pl.ds(pl.multiple_of(i * LANES, LANES), LANES)


def variants(k_blocks, n_blocks, body):
    for k in (1, 2):
        for n in (1, 2):
            @pl.when((k_blocks == k) & (n_blocks == n))
            def _():
                body(k * LANES, n * LANES)


S_PSI, S_PROD, S_TURN, S_RIGHT, STRIPS = 0, 2, 6, 10, 14
TOGETHER = 2


def carry_kernel(sizes, psi_ref, right_ref, strip_ref):
    row = lax.broadcasted_iota(jnp.int32, (BLK, BLK), 0)
    col = lax.broadcasted_iota(jnp.int32, (BLK, BLK), 1)

    def put(i, first, block):
        for strip in range(2):
            strip_ref[i, first + strip] = block[:, strip * LANES : (strip + 1) * LANES]

    for i in range(TOGETHER):
        d = pl.program_id(0) * TOGETHER + i
        kept = (row < sizes[d]) & (col < sizes[HELD + d])
        psi = jnp.where(kept, psi_ref[i], 0.0)
        parts = split3(psi)
        put(i, S_PSI, psi.T)
        for t in range(PAIRS // HELD):
            right = right_ref[t, i]
            product = dot3(parts, split3(right))
            put(i, S_RIGHT + 2 * t, right)
            put(i, S_PROD + 2 * t, product)
            put(i, S_TURN + 2 * t, product.T)


def send_kernel(tbl, strip_ref, buf_ref, held_ref, sems):
    def copy(e):
        return pltpu.make_async_copy(strip_ref.at[tbl[3 * e]], held_ref.at[e], sems.at[e])

    for e in range(4 * PAIRS):
        @pl.when(tbl[3 * e + 1] > 0)
        def _():
            copy(e).start()

    for e in range(4 * PAIRS):
        rows, first = tbl[3 * e + 1], tbl[3 * e + 2]

        @pl.when(rows > 0)
        def _():
            copy(e).wait()

            def four(i, inner):
                for k in range(4):
                    a = i * 4 + k
                    at = tile_rows(first + a, ROWS_OUT)
                    buf_ref[pl.ds(at, ROWS, stride=ROWS_OUT), :] = held_ref[e, tile_at(a), :]
                return inner

            lax.fori_loop(0, (rows + 3) // 4, four, 0)


def relay_kernel(idx, count, in_ref, out_ref):
    def slot(peer, carry):
        def some(i, inner):
            at = peer * ROWS_IN + i * ROWS
            for k in range(ROWS):
                out_ref[pl.ds(at + k, 1), :] = in_ref[pl.ds(idx[at + k], 1), :]
            return inner

        lax.fori_loop(0, (count[peer] + ROWS - 1) // ROWS, some, 0)
        return carry

    lax.fori_loop(0, PEERS, slot, 0)


STREAM = MEMBERS * PIECE


def piece_at(place, core, chip):
    piece = ((place // 4) ^ core) * 4 + ((place % 4) ^ chip)
    return pl.ds(pl.multiple_of(piece * PIECE, PIECE), PIECE)


def land_kernel(
    tbl, out_tbl, buf_ref, left_ref, keep_ref, send_ref, x_ref, y_ref, z_ref, sum_ref, stream_ref
):
    z_ref[...] = jnp.zeros_like(z_ref)

    def take(dst_ref, u, strip, before, rows):
        at = u * T_WIDTH
        start = tbl[at + T_START] + before
        begin = []
        for k in range(4):
            kind = (start + k) % 4
            rank = tbl[at + T_BASE + kind] + (before + k) // 4
            begin.append((kind * (ROWS * ROWS_IN), rank))

        def four(i, carry):
            for k in range(4):
                first, rank = begin[k]
                row = first + jnp.minimum(rank + i, ROWS_IN - 1)
                dst_ref[u, tile_at(i * 4 + k), strip_at(strip)] = buf_ref[
                    pl.ds(row, ROWS, stride=ROWS_IN), :
                ]
            return carry

        lax.fori_loop(0, (rows + 3) // 4, four, 0)

    def unpack(u, carry):
        at = u * T_WIDTH
        rows, nx, ny = tbl[at + T_ROWS], tbl[at + T_NX], tbl[at + T_NY]
        for strip in range(2):
            @pl.when(strip < nx)
            def _():
                take(x_ref, u, strip, strip * rows, rows)

            @pl.when(strip < ny)
            def _():
                take(y_ref, u, strip, (nx + strip) * rows, rows)

        return carry

    lax.fori_loop(0, PAIRS, unpack, 0)

    def blocks(rows):
        return (rows * ROWS + LANES - 1) // LANES

    def sector(d, carry):
        first, out_rows, strips = out_tbl[3 * d], out_tbl[3 * d + 1], out_tbl[3 * d + 2]
        units = [d + t * HELD for t in range(PAIRS // HELD)]
        rows = [tbl[u * T_WIDTH + T_ROWS] for u in units]
        nx = [tbl[u * T_WIDTH + T_NX] for u in units]
        ny = [tbl[u * T_WIDTH + T_NY] for u in units]
        m_blocks = blocks(out_rows)

        def masked(ref, t, height, width, count):
            row = lax.broadcasted_iota(jnp.int32, (height, width), 0)
            col = lax.broadcasted_iota(jnp.int32, (height, width), 1)
            kept = (row < rows[t] * ROWS) & (col < count * LANES)
            return jnp.where(kept, ref[units[t], :height, :width], 0.0)

        def turned(k, n):
            mats = [split3(masked(x_ref, t, n, k, nx[t])) for t in range(2)]

            def some(i, inner):
                for t in range(2):
                    z_ref[t, block_at(i), :n] = dot3(
                        split3(left_ref[units[t], block_at(i), :k]), mats[t], transposed=True
                    )
                return inner

            lax.fori_loop(0, m_blocks, some, 0)

        inner_x = [jnp.where(nx[t] > 0, blocks(rows[t]), 0) for t in range(2)]
        variants(jnp.maximum(nx[0], nx[1]), jnp.maximum(inner_x[0], inner_x[1]), turned)

        def added(k, n):
            mats = [split3(masked(y_ref, t, k, n, ny[t])) for t in range(2)]

            def some(i, inner):
                total = None
                for t in range(2):
                    a = jnp.where(
                        nx[t] > 0, z_ref[t, block_at(i), :k], left_ref[units[t], block_at(i), :k]
                    )
                    part = dot3(split3(a), mats[t]) + jnp.where(
                        ny[t] > 0, 0.0, z_ref[t, block_at(i), :n]
                    )
                    total = part if total is None else total + part
                sum_ref[block_at(i), :n] = total
                return inner

            lax.fori_loop(0, m_blocks, some, 0)

        inner_y = [jnp.where(ny[t] > 0, blocks(rows[t]), 1) for t in range(2)]
        variants(jnp.maximum(inner_y[0], inner_y[1]), strips, added)

        for strip in range(2):
            @pl.when(strip < strips)
            def _():
                begin = first + strip * out_rows

                def four(i, inner):
                    at = jnp.minimum(begin + i * 4, STREAM)
                    for k in range(4):
                        stream_ref[at + k] = sum_ref[tile_at(i * 4 + k), strip_at(strip)]
                    return inner

                lax.fori_loop(0, (out_rows + 3) // 4, four, 0)
        return carry

    lax.fori_loop(0, HELD, sector, 0)
    core, chip = out_tbl[O_CORE], out_tbl[O_CHIP]
    flag = jnp.full((ROWS, LANES), out_tbl[O_FLAG], jnp.int32).astype(jnp.float32)
    stream_ref[STREAM - 1] = flag
    for place in range(4):
        into = pl.ds(place * PIECE, PIECE)
        keep_ref[into] = stream_ref[piece_at(place, core, chip)]
        send_ref[into] = stream_ref[piece_at(place + 4, core, chip)]


def spread_kernel(out_tbl, sizes, own_ref, other_ref, out_ref, flag_ref, stream_ref):
    d = pl.program_id(0)

    @pl.when(d == 0)
    def _():
        core, chip = out_tbl[O_CORE], out_tbl[O_CHIP]
        for place in range(4):
            part = pl.ds(place * PIECE, PIECE)
            stream_ref[piece_at(place, core, chip)] = own_ref[part]
            stream_ref[piece_at(place + 4, core, chip)] = other_ref[part]
        flag_ref[0] = jnp.max(stream_ref[STREAM - 1])

    row = lax.broadcasted_iota(jnp.int32, (ROWS, LANES), 0)
    col = lax.broadcasted_iota(jnp.int32, (ROWS, LANES), 1)
    out_ref[...] = jnp.zeros_like(out_ref)
    first, rows, strips = out_tbl[3 * d], out_tbl[3 * d + 1], out_tbl[3 * d + 2]
    height, width = sizes[d], sizes[HELD + d]
    for strip in range(2):
        @pl.when(strip < strips)
        def _():
            begin = first + strip * rows
            col_ok = col + strip * LANES < width

            def four(i, inner):
                at = jnp.minimum(begin + i * 4, STREAM)
                for k in range(4):
                    a = i * 4 + k
                    kept = col_ok & (row + a * ROWS < height)
                    tile = jnp.where(kept, stream_ref[at + k], 0.0)
                    out_ref[0, tile_at(a), strip_at(strip)] = tile
                return inner

            lax.fori_loop(0, (rows + 3) // 4, four, 0)


O_CORE, O_CHIP, O_FLAG = 3 * HELD, 3 * HELD + 1, 3 * HELD + 2

SMEM = pl.BlockSpec(memory_space=pltpu.SMEM)
VMEM = pl.BlockSpec(memory_space=pltpu.VMEM)
PARAMS = pltpu.CompilerParams(vmem_limit_bytes=VMEM_BYTES)
WIDE = pltpu.CompilerParams(vmem_limit_bytes=WIDE_BYTES)


def floats(*shape):
    return jax.ShapeDtypeStruct(shape, jnp.float32)


def scratch(*shape):
    return pltpu.VMEM(shape, jnp.float32)


def carry_call(sizes, psi, right):
    return pl.pallas_call(
        carry_kernel,
        grid=(HELD // TOGETHER,),
        out_shape=floats(HELD, STRIPS, BLK, LANES),
        in_specs=[
            SMEM,
            pl.BlockSpec((TOGETHER, BLK, BLK), lambda d: (d, 0, 0)),
            pl.BlockSpec((PAIRS // HELD, TOGETHER, BLK, BLK), lambda d: (0, d, 0, 0)),
        ],
        out_specs=pl.BlockSpec((TOGETHER, STRIPS, BLK, LANES), lambda d: (d, 0, 0, 0)),
        cost_estimate=pl.CostEstimate(
            flops=6 * PAIRS * BLK**3, bytes_accessed=24 * 2**20, transcendentals=0
        ),
        compiler_params=WIDE,
    )(sizes, psi, right)


def send_call(tbl, strips):
    return pl.pallas_call(
        send_kernel,
        out_shape=floats(PEERS * ROWS_OUT, LANES),
        in_specs=[SMEM, pl.BlockSpec(memory_space=pl.ANY)],
        out_specs=VMEM,
        scratch_shapes=[
            scratch(4 * PAIRS, BLK, LANES),
            pltpu.SemaphoreType.DMA((4 * PAIRS,)),
        ],
        compiler_params=WIDE,
    )(tbl, strips)


def relay_call(idx, count, received):
    return pl.pallas_call(
        relay_kernel,
        out_shape=floats(PEERS * ROWS_IN, LANES),
        in_specs=[SMEM, SMEM, VMEM],
        out_specs=VMEM,
        compiler_params=PARAMS,
    )(idx, count, received)


def land_call(tbl, out_tbl, received, left):
    return pl.pallas_call(
        land_kernel,
        out_shape=[floats(4 * PIECE, ROWS, LANES)] * 2,
        in_specs=[SMEM, SMEM, VMEM, VMEM],
        out_specs=[VMEM, VMEM],
        scratch_shapes=[
            scratch(PAIRS, BLK, BLK),
            scratch(PAIRS, BLK, BLK),
            scratch(PAIRS // HELD, BLK, BLK),
            scratch(BLK, BLK),
            scratch(STREAM + ROWS, ROWS, LANES),
        ],
        compiler_params=PARAMS,
    )(tbl, out_tbl, received, left)


def spread_call(out_tbl, sizes, own, other):
    return pl.pallas_call(
        spread_kernel,
        grid=(HELD,),
        out_shape=[floats(HELD, BLK, BLK), floats(1)],
        in_specs=[SMEM, SMEM, VMEM, VMEM],
        out_specs=[pl.BlockSpec((1, BLK, BLK), lambda d: (d, 0, 0)), SMEM],
        scratch_shapes=[scratch(STREAM + ROWS, ROWS, LANES)],
        compiler_params=WIDE,
    )(out_tbl, sizes, own, other)


def up(value, unit):
    return (value + (unit - 1)) // unit


def before(values, axis):
    n = values.shape[axis]
    moved = jnp.moveaxis(values, axis, -1)
    lower = jnp.arange(n)[:, None] > jnp.arange(n)[None, :]
    total = jnp.sum(jnp.where(lower, moved[..., None, :], 0), axis=-1)
    return jnp.moveaxis(total, -1, axis)


def make_tables(facts, me, core, chip):
    size_l, size_r = facts[:, 0], facts[:, 1]
    dest = facts[:, 2:].reshape(PEERS, PAIRS)

    ls = jnp.concatenate([size_l, size_l], axis=1)
    rs = jnp.concatenate([size_r, size_r], axis=1)
    to_dev = dest // HELD
    hit_dev = to_dev[:, :, None] == jnp.arange(PEERS)[None, None, :]
    sector = jnp.arange(PEERS * HELD)[:, None]
    rd = jnp.sum(
        jnp.where(dest.reshape(1, -1) == sector, size_r.reshape(-1)[:, None], 0), axis=0
    ).reshape(PEERS, PAIRS)
    nl, nr = up(ls, LANES), up(rd, LANES)
    cost_c = up(ls, ROWS) * nr
    cost_ct = up(rd, ROWS) * nl
    cost_f = up(rs, ROWS) * (nl + nr)
    is_f = (cost_f < cost_c) & (cost_f < cost_ct)
    is_ct = ~is_f & (cost_ct < cost_c)
    rows = up(jnp.where(is_f, rs, jnp.where(is_ct, rd, ls)), ROWS)
    nx = jnp.where(is_f | is_ct, nl, 0)
    ny = jnp.where(is_ct, 0, nr)
    tiles = rows * (nx + ny)
    start = before(tiles, 1)
    total = jnp.sum(tiles, axis=1)

    kinds = jnp.arange(4)[:, None, None]
    lag = (kinds - start) % 4
    share = (tiles + 3 - lag) // 4
    first_row = (start + lag) // 4
    onto = jnp.sum(jnp.where(hit_dev[None], share[..., None], 0), axis=2)
    base = before(onto, 1)
    filled = jnp.sum(onto, axis=1)

    out_rows, out_strips = up(size_l, ROWS), up(size_r, LANES)
    out_tiles = out_rows * out_strips
    out_first = before(out_tiles, 1)
    spilled = (
        jnp.any(total > 4 * (ROWS_OUT - 1))
        | jnp.any(filled > ROWS_IN)
        | jnp.any(jnp.sum(out_tiles, axis=1) > MEMBERS * PIECE - 1)
    )

    def own(values, axis=0):
        return lax.dynamic_index_in_dim(values, me, axis, keepdims=False)

    pair, place = jnp.arange(PAIRS)[:, None], jnp.arange(4)[None, :]
    own_nx, own_ny, own_rows = own(nx)[:, None], own(ny)[:, None], own(rows)[:, None]
    both = (own_nx > 0) & (own_ny > 0)
    term, held = pair // HELD, pair % HELD
    source = jnp.where(
        place < 2,
        jnp.where(both, S_PSI, S_TURN + 2 * term),
        jnp.where(both, S_RIGHT, S_PROD) + 2 * term,
    )
    source = held * STRIPS + source + place % 2
    used = jnp.where(place < 2, place < own_nx, place - 2 < own_ny)
    index = jnp.where(place < 2, place, own_nx + place - 2)
    send_tbl = jnp.stack(
        [source, jnp.where(used, own_rows, 0), own(start)[:, None] + index * own_rows], axis=2
    ).reshape(-1)

    kind = me // ROWS
    onto_k = lax.dynamic_index_in_dim(onto, kind, 0, keepdims=False)
    base_k = lax.dynamic_index_in_dim(base, kind, 0, keepdims=False)
    first_k = lax.dynamic_index_in_dim(first_row, kind, 0, keepdims=False)
    filled_k = lax.dynamic_index_in_dim(filled, kind, 0, keepdims=False)
    first_to = jnp.sum(jnp.where(hit_dev, first_k[:, :, None], 0), axis=1)
    rank = jnp.arange(ROWS_IN)[None, None, :]
    here = (rank >= base_k[:, :, None]) & (rank < (base_k + onto_k)[:, :, None])
    origin = jnp.arange(PEERS)[:, None] * ROWS_OUT + first_to - base_k
    relay_idx = jnp.sum(jnp.where(here, origin[:, :, None] + rank, 0), axis=0)
    relay_idx = jnp.clip(relay_idx, 0, PEERS * ROWS_OUT - 1).reshape(-1)
    relay_count = jnp.minimum(filled_k, ROWS_IN)

    unit = jnp.arange(PAIRS)[:, None, None]
    reach = (dest[None] == me * HELD + unit % HELD) & (
        (jnp.arange(PAIRS) // HELD)[None, None, :] == unit // HELD
    )

    def reached(values):
        return jnp.sum(jnp.where(reach, values[None], 0), axis=(1, 2))

    base_me = lax.dynamic_index_in_dim(base, me, 2, keepdims=False)
    land_tbl = jnp.stack(
        [reached(start), reached(rows), reached(nx), reached(ny), reached(ls), reached(rs)]
        + [reached(jnp.broadcast_to(base_me[g][:, None], (PEERS, PAIRS))) for g in range(4)],
        axis=1,
    ).reshape(-1)

    out_tbl = jnp.concatenate(
        [
            jnp.stack([own(out_first), own(out_rows), own(out_strips)], axis=1).reshape(-1),
            jnp.stack([core, chip, spilled.astype(jnp.int32)]).astype(jnp.int32),
        ]
    )
    return send_tbl, relay_idx, relay_count, land_tbl, out_tbl


def per_device(psi_blocks, left_env, right_env, left_sizes, right_sizes, dest_sector):
    me = lax.axis_index("sec")
    member = lax.axis_index("term")
    core, chip = member % 2, member // 2
    sizes = jnp.concatenate([left_sizes, right_sizes])
    strips = carry_call(sizes, psi_blocks, right_env).reshape(HELD * STRIPS, BLK, LANES)
    mine = jnp.concatenate([left_sizes[None], right_sizes[None], dest_sector])
    facts = lax.all_to_all(
        jnp.broadcast_to(mine[None], (PEERS, 4, HELD)), "sec", 0, 0, tiled=True
    )
    tables = make_tables(facts, me, core, chip)
    send_tbl, relay_idx, relay_count, land_tbl, out_tbl = tables

    sent = send_call(send_tbl, strips)
    hop = lax.all_to_all(sent.reshape(PEERS, ROWS_OUT, LANES), "sec", 0, 0, tiled=True)
    passed = relay_call(relay_idx, relay_count, hop.reshape(PEERS * ROWS_OUT, LANES))
    hop = lax.all_to_all(passed.reshape(PEERS, ROWS_IN, LANES), "sec", 0, 0, tiled=True)
    keep, give = land_call(
        land_tbl,
        out_tbl,
        hop.reshape(PEERS * ROWS_IN, LANES),
        left_env.reshape(PAIRS, BLK, BLK),
    )

    def swap(values, bits):
        return lax.ppermute(values, "term", [(i, i ^ bits) for i in range(MEMBERS)])

    half = (keep + swap(give, 1)).reshape(4, PIECE, ROWS, LANES)
    piece = half[0] + swap(half[1], 2) + swap(half[2], 4) + swap(half[3], 6)
    whole = jnp.concatenate([piece, swap(piece, 2), swap(piece, 4), swap(piece, 6)])
    other = swap(whole, 1)

    packed, flag = spread_call(out_tbl, sizes, whole, other)
    return lax.cond(
        flag[0] > 0.5,
        lambda: dense_program(
            psi_blocks, left_env, right_env, left_sizes, right_sizes, dest_sector
        ),
        lambda: packed,
    )


def solution(mesh):
    in_specs = (
        P("sec", None, None),
        P("term", "sec", None, None),
        P("term", "sec", None, None),
        P("sec"),
        P("sec"),
        P("term", "sec"),
    )
    out_specs = P("sec", None, None)
    return jax.shard_map(
        per_device, mesh=mesh, in_specs=in_specs, out_specs=out_specs, check_vma=False
    )
```

```python
import functools
import jax
import jax.numpy as jnp
import numpy as np
from jax import lax
from jax.experimental import pallas as pl
from jax.experimental.pallas import tpu as pltpu
from jax.sharding import PartitionSpec as P

BLK = 256
LANES = 128
ROWS = 8
PEERS = 32
MEMBERS = 8
HELD = 8
PAIRS = 16
ROWS_OUT = 64
ROWS_IN = 64
PIECE = 32
VMEM_BYTES = 24 * 1024 * 1024
WIDE_BYTES = 56 * 1024 * 1024
WIDEST_BYTES = 62 * 1024 * 1024


def sector_mask(left_sizes, right_sizes, block_size):
    positions = jnp.arange(block_size, dtype=jnp.int32)
    row_ok = positions[None, :, None] < left_sizes[:, None, None]
    col_ok = positions[None, None, :] < right_sizes[:, None, None]
    return (row_ok & col_ok).astype(jnp.float32)


def pack_blocks(outgoing, targets, term_ids, sector_local, capacity, slot_count):
    target_device = targets // sector_local
    target_place = targets % sector_local
    count_out = targets.shape[0]
    order_index = jnp.arange(count_out, dtype=jnp.int32)
    same_device = target_device[:, None] == target_device[None, :]
    earlier = order_index[None, :] < order_index[:, None]
    peer_rank = jnp.sum((same_device & earlier).astype(jnp.int32), axis=1)
    send_slot = target_device * capacity + peer_rank
    chosen = jnp.arange(slot_count, dtype=jnp.int32)[:, None] == send_slot[None, :]
    slot_source = jnp.sum(jnp.where(chosen, order_index[None, :], 0), axis=1)
    filled = jnp.any(chosen, axis=1)
    buffer = jnp.where(filled[:, None, None], outgoing[slot_source], 0.0)
    left_code = term_ids * sector_local + target_place
    meta_codes = jnp.where(filled, left_code[slot_source], -1)
    return (buffer, meta_codes)


def apply_left(received, meta_codes, flat_left, sector_local, live_count):
    slot_count = meta_codes.shape[0]
    is_valid = meta_codes >= 0
    live_rank = jnp.cumsum(is_valid.astype(jnp.int32)) - 1
    wanted = jnp.arange(live_count, dtype=jnp.int32)
    picked = (live_rank[None, :] == wanted[:, None]) & is_valid[None, :]
    slot_index = jnp.arange(slot_count, dtype=jnp.int32)
    source_slot = jnp.sum(jnp.where(picked, slot_index[None, :], 0), axis=1)
    compact_blocks = received[source_slot]
    compact_codes = meta_codes[source_slot]
    chosen_left = flat_left[compact_codes]
    landed = jnp.einsum(
        "pab,pbc->pac", chosen_left, compact_blocks, precision=lax.Precision.HIGHEST
    )
    target_place = compact_codes % sector_local
    onehot_place = target_place[:, None] == jnp.arange(sector_local, dtype=jnp.int32)[None, :]
    return jnp.einsum(
        "pk,pac->kac", onehot_place.astype(jnp.float32), landed, precision=lax.Precision.HIGHEST
    )


def dense_program(psi_blocks, left_env, right_env, left_sizes, right_sizes, dest_sector):
    term_local = left_env.shape[0]
    sector_local = left_env.shape[1]
    block_size = left_env.shape[2]
    peers = lax.axis_size("sec")
    capacity = (term_local * sector_local + peers - 1) // peers
    slot_count = peers * capacity
    valid_mask = sector_mask(left_sizes, right_sizes, block_size)
    masked_psi = psi_blocks * valid_mask
    carried = jnp.einsum("sab,tsbc->tsac", masked_psi, right_env, precision=lax.Precision.HIGHEST)
    flat_left = left_env.reshape(term_local * sector_local, block_size, block_size)
    term_ids = jnp.repeat(jnp.arange(term_local, dtype=jnp.int32), sector_local)
    buffer, meta_codes = pack_blocks(
        carried.reshape(term_local * sector_local, block_size, block_size),
        dest_sector.reshape(term_local * sector_local),
        term_ids,
        sector_local,
        capacity,
        slot_count,
    )
    received, codes_in = (
        lax.all_to_all(buffer, "sec", split_axis=0, concat_axis=0, tiled=True),
        lax.all_to_all(meta_codes, "sec", split_axis=0, concat_axis=0, tiled=True),
    )
    partial_sum = apply_left(received, codes_in, flat_left, sector_local, term_local * sector_local)
    total = lax.psum(partial_sum, "term")
    return total * valid_mask


def split3(a):
    hi = a.astype(jnp.bfloat16)
    lo = (a - hi.astype(jnp.float32)).astype(jnp.bfloat16)
    return hi, lo


def dot3(a, b, transposed=False):
    dims = (((1,), (1 if transposed else 0,)), ((), ()))
    mul = functools.partial(
        lax.dot_general, dimension_numbers=dims, preferred_element_type=jnp.float32
    )
    return mul(a[0], b[0]) + (mul(a[0], b[1]) + mul(a[1], b[0]))


T_START, T_ROWS, T_NX, T_NY, T_LEFT, T_RIGHT, T_BASE = 0, 1, 2, 3, 4, 5, 6
T_WIDTH = 10


def tile_rows(stream, rows):
    return (stream & 3) * (ROWS * rows) + jnp.minimum(stream >> 2, rows - 1)


def tile_at(a):
    return pl.ds(pl.multiple_of(a * ROWS, ROWS), ROWS)


def strip_at(strip):
    return pl.ds(strip * LANES, LANES)


def block_at(i):
    return pl.ds(pl.multiple_of(i * LANES, LANES), LANES)


def variants(m_blocks, k_blocks, n_blocks, body):
    code = m_blocks * 4 + k_blocks * 2 + n_blocks - 7
    for m in (1, 2):
        for k in (1, 2):
            for n in (1, 2):
                @pl.when((code == m * 4 + k * 2 + n - 7) & (k_blocks > 0))
                def _():
                    body(m * LANES, k * LANES, n * LANES)


S_PSI, S_PROD, S_TURN, S_RIGHT, STRIPS = 0, 2, 6, 10, 14
TOGETHER = 2


def carry_kernel(left_sizes, right_sizes, psi_ref, right_ref, strip_ref):
    row = lax.broadcasted_iota(jnp.int32, (BLK, BLK), 0)
    col = lax.broadcasted_iota(jnp.int32, (BLK, BLK), 1)

    def put(i, first, block):
        for strip in range(2):
            strip_ref[i, first + strip] = block[:, strip * LANES : (strip + 1) * LANES]

    for i in range(TOGETHER):
        d = pl.program_id(0) * TOGETHER + i
        kept = (row < left_sizes[d]) & (col < right_sizes[d])
        psi = jnp.where(kept, psi_ref[i], 0.0)
        parts = split3(psi)
        put(i, S_PSI, psi.T)
        for t in range(PAIRS // HELD):
            right = right_ref[t, i]
            product = dot3(parts, split3(right))
            put(i, S_RIGHT + 2 * t, right)
            put(i, S_PROD + 2 * t, product)
            put(i, S_TURN + 2 * t, product.T)


def send_kernel(source, rows, first, strip_ref, buf_ref, held_ref, sems):
    def copy(p, c):
        e = 4 * p + c
        return pltpu.make_async_copy(strip_ref.at[source[p, c]], held_ref.at[e], sems.at[e])

    places = [(p, c) for p in range(PAIRS) for c in range(4)]
    for p, c in places:
        @pl.when(rows[p, c] > 0)
        def _():
            copy(p, c).start()

    for p, c in places:
        @pl.when(rows[p, c] > 0)
        def _():
            copy(p, c).wait()
            begin = first[p, c]

            def four(i, inner):
                for k in range(4):
                    a = i * 4 + k
                    at = tile_rows(begin + a, ROWS_OUT)
                    tile = held_ref[4 * p + c, tile_at(a), :]
                    buf_ref[pl.ds(at, ROWS, stride=ROWS_OUT), :] = tile
                return inner

            lax.fori_loop(0, (rows[p, c] + 3) >> 2, four, 0)


def relay_kernel(idx, count, in_ref, out_ref):
    def slot(peer, carry):
        def some(i, inner):
            at = peer * ROWS_IN + i * ROWS
            for k in range(ROWS):
                out_ref[pl.ds(at + k, 1), :] = in_ref[pl.ds(idx[at + k], 1), :]
            return inner

        lax.fori_loop(0, (count[peer] + ROWS - 1) >> 3, some, 0)
        return carry

    lax.fori_loop(0, PEERS, slot, 0)


STREAM = MEMBERS * PIECE
SENT = PIECE + 1


def piece_at(place, core, chip):
    piece = ((place >> 2) ^ core) * 4 + ((place & 3) ^ chip)
    return pl.ds(pl.multiple_of(piece * PIECE, PIECE), PIECE)


def land_kernel(
    tbl, out_tbl, buf_ref, left_ref, keep_ref, send_ref, x_ref, y_ref, z_ref, sum_ref, stream_ref
):
    z_ref[...] = jnp.zeros_like(z_ref)

    def take(dst_ref, u, strip, before, rows):
        at = u * T_WIDTH
        start = tbl[at + T_START] + before
        begin = []
        for k in range(4):
            kind = (start + k) & 3
            rank = tbl[at + T_BASE + kind] + ((before + k) >> 2)
            begin.append((kind * (ROWS * ROWS_IN), rank))

        def four(i, carry):
            for k in range(4):
                first, rank = begin[k]
                row = first + jnp.minimum(rank + i, ROWS_IN - 1)
                dst_ref[u, tile_at(i * 4 + k), strip_at(strip)] = buf_ref[
                    pl.ds(row, ROWS, stride=ROWS_IN), :
                ]
            return carry

        lax.fori_loop(0, (rows + 3) >> 2, four, 0)

    def unpack(u, carry):
        at = u * T_WIDTH
        rows, nx, ny = tbl[at + T_ROWS], tbl[at + T_NX], tbl[at + T_NY]
        for strip in range(2):
            @pl.when(strip < nx)
            def _():
                take(x_ref, u, strip, strip * rows, rows)

            @pl.when(strip < ny)
            def _():
                take(y_ref, u, strip, (nx + strip) * rows, rows)

        return carry

    lax.fori_loop(0, PAIRS, unpack, 0)

    def blocks(rows):
        return (rows * ROWS + LANES - 1) >> 7

    def sector(d, carry):
        first, out_rows, strips = out_tbl[3 * d], out_tbl[3 * d + 1], out_tbl[3 * d + 2]
        units = [d + t * HELD for t in range(PAIRS // HELD)]
        rows = [tbl[u * T_WIDTH + T_ROWS] for u in units]
        nx = [tbl[u * T_WIDTH + T_NX] for u in units]
        ny = [tbl[u * T_WIDTH + T_NY] for u in units]
        m_blocks = blocks(out_rows)

        def masked(ref, t, height, width, count):
            row = lax.broadcasted_iota(jnp.int32, (height, width), 0)
            col = lax.broadcasted_iota(jnp.int32, (height, width), 1)
            kept = (row < rows[t] * ROWS) & (col < count * LANES)
            return jnp.where(kept, ref[units[t], :height, :width], 0.0)

        def turned(m, k, n):
            for t in range(2):
                z_ref[t, :m, :n] = dot3(
                    split3(left_ref[units[t], :m, :k]),
                    split3(masked(x_ref, t, n, k, nx[t])),
                    transposed=True,
                )

        inner_x = [jnp.where(nx[t] > 0, blocks(rows[t]), 0) for t in range(2)]
        variants(
            m_blocks, jnp.maximum(nx[0], nx[1]), jnp.maximum(inner_x[0], inner_x[1]), turned
        )

        def added(m, k, n):
            total = None
            for t in range(2):
                a = jnp.where(nx[t] > 0, z_ref[t, :m, :k], left_ref[units[t], :m, :k])
                part = dot3(split3(a), split3(masked(y_ref, t, k, n, ny[t])))
                part = part + jnp.where(ny[t] > 0, 0.0, z_ref[t, :m, :n])
                total = part if total is None else total + part
            sum_ref[:m, :n] = total

        inner_y = [jnp.where(ny[t] > 0, blocks(rows[t]), 1) for t in range(2)]
        variants(m_blocks, jnp.maximum(inner_y[0], inner_y[1]), strips, added)

        for strip in range(2):
            @pl.when(strip < strips)
            def _():
                begin = first + strip * out_rows

                def four(i, inner):
                    at = jnp.minimum(begin + i * 4, STREAM)
                    for k in range(4):
                        stream_ref[at + k] = sum_ref[tile_at(i * 4 + k), strip_at(strip)]
                    return inner

                lax.fori_loop(0, (out_rows + 3) >> 2, four, 0)
        return carry

    lax.fori_loop(0, HELD, sector, 0)
    core, chip = out_tbl[O_CORE], out_tbl[O_CHIP]
    flag = jnp.full((ROWS, LANES), out_tbl[O_FLAG], jnp.int32).astype(jnp.float32)
    for place in range(4):
        into = pl.ds(place * SENT, PIECE)
        keep_ref[into] = stream_ref[piece_at(place, core, chip)]
        send_ref[into] = stream_ref[piece_at(place + 4, core, chip)]
        keep_ref[place * SENT + PIECE] = flag
        send_ref[place * SENT + PIECE] = flag


def spread_kernel(
    out_tbl, left_sizes, right_sizes, own_ref, other_ref, out_ref, stream_ref, block_ref, sems
):
    core, chip = out_tbl[O_CORE], out_tbl[O_CHIP]
    for place in range(4):
        part = pl.ds(place * SENT, PIECE)
        stream_ref[piece_at(place, core, chip)] = own_ref[part]
        stream_ref[piece_at(place + 4, core, chip)] = other_ref[part]

    row = lax.broadcasted_iota(jnp.int32, (ROWS, LANES), 0)
    col = lax.broadcasted_iota(jnp.int32, (ROWS, LANES), 1)
    copies = []
    for d in range(HELD):
        block_ref[d] = jnp.zeros((BLK, BLK), jnp.float32)
        first, rows, strips = out_tbl[3 * d], out_tbl[3 * d + 1], out_tbl[3 * d + 2]
        height, width = left_sizes[d], right_sizes[d]
        for strip in range(2):
            @pl.when(strip < strips)
            def _():
                begin = first + strip * rows
                col_ok = col + strip * LANES < width

                def four(i, inner):
                    at = jnp.minimum(begin + i * 4, STREAM)
                    for k in range(4):
                        a = i * 4 + k
                        kept = col_ok & (row + a * ROWS < height)
                        tile = jnp.where(kept, stream_ref[at + k], 0.0)
                        block_ref[d, tile_at(a), strip_at(strip)] = tile
                    return inner

                lax.fori_loop(0, (rows + 3) >> 2, four, 0)

        copies.append(pltpu.make_async_copy(block_ref.at[d], out_ref.at[d], sems.at[d]))
        copies[-1].start()
    for copy in copies:
        copy.wait()


O_CORE, O_CHIP, O_FLAG = 3 * HELD, 3 * HELD + 1, 3 * HELD + 2

SMEM = pl.BlockSpec(memory_space=pltpu.SMEM)
VMEM = pl.BlockSpec(memory_space=pltpu.VMEM)
PARAMS = pltpu.CompilerParams(vmem_limit_bytes=VMEM_BYTES)
WIDEST = pltpu.CompilerParams(vmem_limit_bytes=WIDEST_BYTES)
WIDE = pltpu.CompilerParams(vmem_limit_bytes=WIDE_BYTES)


def floats(*shape):
    return jax.ShapeDtypeStruct(shape, jnp.float32)


def scratch(*shape):
    return pltpu.VMEM(shape, jnp.float32)


def carry_call(left_sizes, right_sizes, psi, right):
    return pl.pallas_call(
        carry_kernel,
        grid=(HELD // TOGETHER,),
        out_shape=floats(HELD, STRIPS, BLK, LANES),
        in_specs=[
            SMEM,
            SMEM,
            pl.BlockSpec((TOGETHER, BLK, BLK), lambda d: (d, 0, 0)),
            pl.BlockSpec((PAIRS // HELD, TOGETHER, BLK, BLK), lambda d: (0, d, 0, 0)),
        ],
        out_specs=pl.BlockSpec((TOGETHER, STRIPS, BLK, LANES), lambda d: (d, 0, 0, 0)),
        cost_estimate=pl.CostEstimate(
            flops=6 * PAIRS * BLK**3, bytes_accessed=24 * 2**20, transcendentals=0
        ),
        compiler_params=WIDE,
    )(left_sizes, right_sizes, psi, right)


def send_call(tables, strips):
    return pl.pallas_call(
        send_kernel,
        out_shape=floats(PEERS * ROWS_OUT, LANES),
        in_specs=[SMEM, SMEM, SMEM, pl.BlockSpec(memory_space=pl.ANY)],
        out_specs=VMEM,
        scratch_shapes=[
            scratch(4 * PAIRS, BLK, LANES),
            pltpu.SemaphoreType.DMA((4 * PAIRS,)),
        ],
        compiler_params=WIDE,
    )(*tables, strips)


def relay_call(idx, count, received):
    return pl.pallas_call(
        relay_kernel,
        out_shape=floats(PEERS * ROWS_IN, LANES),
        in_specs=[SMEM, SMEM, VMEM],
        out_specs=VMEM,
        compiler_params=PARAMS,
    )(idx, count, received)


def land_call(tbl, out_tbl, received, left):
    return pl.pallas_call(
        land_kernel,
        out_shape=[floats(4 * SENT, ROWS, LANES)] * 2,
        in_specs=[SMEM, SMEM, VMEM, VMEM],
        out_specs=[VMEM, VMEM],
        scratch_shapes=[
            scratch(PAIRS, BLK, BLK),
            scratch(PAIRS, BLK, BLK),
            scratch(PAIRS // HELD, BLK, BLK),
            scratch(BLK, BLK),
            scratch(STREAM + ROWS, ROWS, LANES),
        ],
        compiler_params=PARAMS,
    )(tbl, out_tbl, received, left)


def spread_call(out_tbl, left_sizes, right_sizes, own, other):
    return pl.pallas_call(
        spread_kernel,
        out_shape=floats(HELD, BLK, BLK),
        in_specs=[SMEM, SMEM, SMEM, VMEM, VMEM],
        out_specs=pl.BlockSpec(memory_space=pl.ANY),
        scratch_shapes=[
            scratch(STREAM + ROWS, ROWS, LANES),
            scratch(HELD, BLK, BLK),
            pltpu.SemaphoreType.DMA((HELD,)),
        ],
        compiler_params=WIDEST,
    )(out_tbl, left_sizes, right_sizes, own, other)


def up(value, unit):
    return (value + (unit - 1)) >> (unit.bit_length() - 1)


def before(values, axis):
    n = values.shape[axis]
    moved = jnp.moveaxis(values, axis, -1)
    lower = np.arange(n)[:, None] > np.arange(n)[None, :]
    total = jnp.sum(jnp.where(lower, moved[..., None, :], 0), axis=-1)
    return jnp.moveaxis(total, -1, axis)


def make_tables(facts, me, core, chip):
    size_l, size_r = facts[:, 0], facts[:, 1]
    dest = facts[:, 2:].reshape(PEERS, PAIRS)

    ls = jnp.concatenate([size_l, size_l], axis=1)
    rs = jnp.concatenate([size_r, size_r], axis=1)
    to_dev = dest >> 3
    hit_dev = to_dev[:, :, None] == np.arange(PEERS, dtype=np.int32)[None, None, :]
    sector = np.arange(PEERS * HELD, dtype=np.int32)[:, None]
    rd = jnp.sum(
        jnp.where(dest.reshape(1, -1) == sector, size_r.reshape(-1)[:, None], 0), axis=0
    ).reshape(PEERS, PAIRS)
    nl, nr = up(ls, LANES), up(rd, LANES)
    cost_c = up(ls, ROWS) * nr
    cost_ct = up(rd, ROWS) * nl
    cost_f = up(rs, ROWS) * (nl + nr)
    is_f = (cost_f < cost_c) & (cost_f < cost_ct)
    is_ct = ~is_f & (cost_ct < cost_c)
    rows = up(jnp.where(is_f, rs, jnp.where(is_ct, rd, ls)), ROWS)
    nx = jnp.where(is_f | is_ct, nl, 0)
    ny = jnp.where(is_ct, 0, nr)
    tiles = rows * (nx + ny)
    start = before(tiles, 1)
    total = jnp.sum(tiles, axis=1)

    kinds = np.arange(4, dtype=np.int32)[:, None, None]
    lag = (kinds - start) & 3
    share = (tiles + 3 - lag) >> 2
    first_row = (start + lag) >> 2
    onto = jnp.sum(jnp.where(hit_dev[None], share[..., None], 0), axis=2)
    base = before(onto, 1)
    filled = jnp.sum(onto, axis=1)

    out_rows, out_strips = up(size_l, ROWS), up(size_r, LANES)
    out_tiles = out_rows * out_strips
    out_first = before(out_tiles, 1)
    spilled = (
        jnp.any(total > 4 * (ROWS_OUT - 1))
        | jnp.any(filled > ROWS_IN)
        | jnp.any(jnp.sum(out_tiles, axis=1) > MEMBERS * PIECE)
    )

    def own(values, axis=0):
        return lax.dynamic_index_in_dim(values, me, axis, keepdims=False)

    pair = np.arange(PAIRS, dtype=np.int32)[:, None]
    place = np.arange(4, dtype=np.int32)[None, :]
    own_nx, own_ny, own_rows = own(nx)[:, None], own(ny)[:, None], own(rows)[:, None]
    both = (own_nx > 0) & (own_ny > 0)
    term, held = pair // HELD, pair % HELD
    source = jnp.where(
        place < 2,
        jnp.where(both, S_PSI, S_TURN + 2 * term),
        jnp.where(both, S_RIGHT, S_PROD) + 2 * term,
    )
    source = held * STRIPS + source + place % 2
    used = jnp.where(place < 2, place < own_nx, place - 2 < own_ny)
    index = jnp.where(place < 2, place, own_nx + place - 2)
    send_tbl = (
        source,
        jnp.where(used, own_rows, 0),
        own(start)[:, None] + index * own_rows,
    )

    kind = me >> 3
    onto_k = lax.dynamic_index_in_dim(onto, kind, 0, keepdims=False)
    base_k = lax.dynamic_index_in_dim(base, kind, 0, keepdims=False)
    first_k = lax.dynamic_index_in_dim(first_row, kind, 0, keepdims=False)
    filled_k = lax.dynamic_index_in_dim(filled, kind, 0, keepdims=False)
    first_to = jnp.sum(jnp.where(hit_dev, first_k[:, :, None], 0), axis=1)
    rank = np.arange(ROWS_IN, dtype=np.int32)[None, None, :]
    here = (rank >= base_k[:, :, None]) & (rank < (base_k + onto_k)[:, :, None])
    origin = np.arange(PEERS, dtype=np.int32)[:, None] * ROWS_OUT + first_to - base_k
    relay_idx = jnp.sum(jnp.where(here, origin[:, :, None] + rank, 0), axis=0)
    relay_idx = jnp.clip(relay_idx, 0, PEERS * ROWS_OUT - 1).reshape(-1)
    relay_count = jnp.minimum(filled_k, ROWS_IN)

    unit = np.arange(PAIRS, dtype=np.int32)[:, None, None]
    reach = (dest[None] == me * HELD + unit % HELD) & (
        (np.arange(PAIRS, dtype=np.int32) // HELD)[None, None, :] == unit // HELD
    )

    def reached(values):
        return jnp.sum(jnp.where(reach, values[None], 0), axis=(1, 2))

    base_me = lax.dynamic_index_in_dim(base, me, 2, keepdims=False)
    land_tbl = jnp.stack(
        [reached(start), reached(rows), reached(nx), reached(ny), reached(ls), reached(rs)]
        + [reached(jnp.broadcast_to(base_me[g][:, None], (PEERS, PAIRS))) for g in range(4)],
        axis=1,
    ).reshape(-1)

    out_tbl = jnp.concatenate(
        [
            jnp.stack([own(out_first), own(out_rows), own(out_strips)], axis=1).reshape(-1),
            jnp.stack([core, chip, spilled.astype(jnp.int32)]).astype(jnp.int32),
        ]
    )
    return send_tbl, relay_idx, relay_count, land_tbl, out_tbl


def per_device(psi_blocks, left_env, right_env, left_sizes, right_sizes, dest_sector):
    me = lax.axis_index("sec")
    member = lax.axis_index("term")
    core, chip = member & 1, member >> 1
    strips = carry_call(left_sizes, right_sizes, psi_blocks, right_env)
    strips = strips.reshape(HELD * STRIPS, BLK, LANES)
    mine = jnp.concatenate([left_sizes[None], right_sizes[None], dest_sector])
    mine = jnp.broadcast_to(mine[None], (PEERS, 4, HELD))
    facts = lax.all_to_all(mine, "sec", 0, 0, tiled=True)
    tables = make_tables(facts, me, core, chip)
    send_tbl, relay_idx, relay_count, land_tbl, out_tbl = tables

    sent = send_call(send_tbl, strips)
    hop = lax.all_to_all(sent.reshape(PEERS, ROWS_OUT, LANES), "sec", 0, 0, tiled=True)
    passed = relay_call(relay_idx, relay_count, hop.reshape(PEERS * ROWS_OUT, LANES))
    hop = lax.all_to_all(passed.reshape(PEERS, ROWS_IN, LANES), "sec", 0, 0, tiled=True)
    keep, give = land_call(
        land_tbl,
        out_tbl,
        hop.reshape(PEERS * ROWS_IN, LANES),
        left_env.reshape(PAIRS, BLK, BLK),
    )

    def swap(values, bits):
        return lax.ppermute(values, "term", [(i, i ^ bits) for i in range(MEMBERS)])

    half = (keep + swap(give, 1)).reshape(4, SENT, ROWS, LANES)
    piece = half[0] + swap(half[1], 2) + swap(half[2], 4) + swap(half[3], 6)
    whole = jnp.concatenate([piece, swap(piece, 2), swap(piece, 4), swap(piece, 6)])
    other = swap(whole, 1)

    return lax.cond(
        piece[PIECE, 0, 0] > 0.5,
        lambda: dense_program(
            psi_blocks, left_env, right_env, left_sizes, right_sizes, dest_sector
        ),
        lambda: spread_call(out_tbl, left_sizes, right_sizes, whole, other),
    )


def solution(mesh):
    in_specs = (
        P("sec", None, None),
        P("term", "sec", None, None),
        P("term", "sec", None, None),
        P("sec"),
        P("sec"),
        P("term", "sec"),
    )
    out_specs = P("sec", None, None)
    return jax.shard_map(
        per_device, mesh=mesh, in_specs=in_specs, out_specs=out_specs, check_vma=False
    )
```

```python
import functools
import jax
import jax.numpy as jnp
import numpy as np
from jax import lax
from jax.experimental import pallas as pl
from jax.experimental.pallas import tpu as pltpu
from jax.sharding import PartitionSpec as P

BLK = 256
LANES = 128
ROWS = 8
PEERS = 32
MEMBERS = 8
HELD = 8
PAIRS = 16
ROWS_OUT = 64
ROWS_IN = 64
PIECE = 24
VMEM_BYTES = 24 * 1024 * 1024
WIDE_BYTES = 56 * 1024 * 1024
WIDEST_BYTES = 62 * 1024 * 1024
SEND_BYTES = 50 * 1024 * 1024


def sector_mask(left_sizes, right_sizes, block_size):
    positions = jnp.arange(block_size, dtype=jnp.int32)
    row_ok = positions[None, :, None] < left_sizes[:, None, None]
    col_ok = positions[None, None, :] < right_sizes[:, None, None]
    return (row_ok & col_ok).astype(jnp.float32)


def pack_blocks(outgoing, targets, term_ids, sector_local, capacity, slot_count):
    target_device = targets // sector_local
    target_place = targets % sector_local
    count_out = targets.shape[0]
    order_index = jnp.arange(count_out, dtype=jnp.int32)
    same_device = target_device[:, None] == target_device[None, :]
    earlier = order_index[None, :] < order_index[:, None]
    peer_rank = jnp.sum((same_device & earlier).astype(jnp.int32), axis=1)
    send_slot = target_device * capacity + peer_rank
    chosen = jnp.arange(slot_count, dtype=jnp.int32)[:, None] == send_slot[None, :]
    slot_source = jnp.sum(jnp.where(chosen, order_index[None, :], 0), axis=1)
    filled = jnp.any(chosen, axis=1)
    buffer = jnp.where(filled[:, None, None], outgoing[slot_source], 0.0)
    left_code = term_ids * sector_local + target_place
    meta_codes = jnp.where(filled, left_code[slot_source], -1)
    return (buffer, meta_codes)


def apply_left(received, meta_codes, flat_left, sector_local, live_count):
    slot_count = meta_codes.shape[0]
    is_valid = meta_codes >= 0
    live_rank = jnp.cumsum(is_valid.astype(jnp.int32)) - 1
    wanted = jnp.arange(live_count, dtype=jnp.int32)
    picked = (live_rank[None, :] == wanted[:, None]) & is_valid[None, :]
    slot_index = jnp.arange(slot_count, dtype=jnp.int32)
    source_slot = jnp.sum(jnp.where(picked, slot_index[None, :], 0), axis=1)
    compact_blocks = received[source_slot]
    compact_codes = meta_codes[source_slot]
    chosen_left = flat_left[compact_codes]
    landed = jnp.einsum(
        "pab,pbc->pac", chosen_left, compact_blocks, precision=lax.Precision.HIGHEST
    )
    target_place = compact_codes % sector_local
    onehot_place = target_place[:, None] == jnp.arange(sector_local, dtype=jnp.int32)[None, :]
    return jnp.einsum(
        "pk,pac->kac", onehot_place.astype(jnp.float32), landed, precision=lax.Precision.HIGHEST
    )


def dense_program(psi_blocks, left_env, right_env, left_sizes, right_sizes, dest_sector):
    term_local = left_env.shape[0]
    sector_local = left_env.shape[1]
    block_size = left_env.shape[2]
    peers = lax.axis_size("sec")
    capacity = (term_local * sector_local + peers - 1) // peers
    slot_count = peers * capacity
    valid_mask = sector_mask(left_sizes, right_sizes, block_size)
    masked_psi = psi_blocks * valid_mask
    carried = jnp.einsum("sab,tsbc->tsac", masked_psi, right_env, precision=lax.Precision.HIGHEST)
    flat_left = left_env.reshape(term_local * sector_local, block_size, block_size)
    term_ids = jnp.repeat(jnp.arange(term_local, dtype=jnp.int32), sector_local)
    buffer, meta_codes = pack_blocks(
        carried.reshape(term_local * sector_local, block_size, block_size),
        dest_sector.reshape(term_local * sector_local),
        term_ids,
        sector_local,
        capacity,
        slot_count,
    )
    received, codes_in = (
        lax.all_to_all(buffer, "sec", split_axis=0, concat_axis=0, tiled=True),
        lax.all_to_all(meta_codes, "sec", split_axis=0, concat_axis=0, tiled=True),
    )
    partial_sum = apply_left(received, codes_in, flat_left, sector_local, term_local * sector_local)
    total = lax.psum(partial_sum, "term")
    return total * valid_mask


def split3(a):
    hi = a.astype(jnp.bfloat16)
    lo = (a - hi.astype(jnp.float32)).astype(jnp.bfloat16)
    return hi, lo


def dot3(a, b, transposed=False):
    dims = (((1,), (1 if transposed else 0,)), ((), ()))
    mul = functools.partial(
        lax.dot_general, dimension_numbers=dims, preferred_element_type=jnp.float32
    )
    return mul(a[0], b[0]) + (mul(a[0], b[1]) + mul(a[1], b[0]))


T_START, T_ROWS, T_NX, T_NY, T_LEFT, T_RIGHT, T_BASE = 0, 1, 2, 3, 4, 5, 6
T_WIDTH = 10


def tile_rows(stream, rows):
    return (stream & 3) * (ROWS * rows) + jnp.minimum(stream >> 2, rows - 1)


def tile_at(a):
    return pl.ds(pl.multiple_of(a * ROWS, ROWS), ROWS)


def strip_at(strip):
    return pl.ds(strip * LANES, LANES)


def block_at(i):
    return pl.ds(pl.multiple_of(i * LANES, LANES), LANES)


def variants(m_blocks, k_blocks, n_blocks, body):
    code = m_blocks * 4 + k_blocks * 2 + n_blocks - 7
    for m in (1, 2):
        for k in (1, 2):
            for n in (1, 2):
                @pl.when((code == m * 4 + k * 2 + n - 7) & (k_blocks > 0))
                def _():
                    body(m * LANES, k * LANES, n * LANES)


S_PSI, S_PROD, S_TURN, S_RIGHT, STRIPS = 0, 2, 6, 10, 14
TOGETHER = 2


def carry_kernel(left_sizes, right_sizes, psi_ref, right_ref, strip_ref):
    row = lax.broadcasted_iota(jnp.int32, (BLK, BLK), 0)
    col = lax.broadcasted_iota(jnp.int32, (BLK, BLK), 1)

    def put(i, first, block):
        for strip in range(2):
            strip_ref[i, first + strip] = block[:, strip * LANES : (strip + 1) * LANES]

    for i in range(TOGETHER):
        d = pl.program_id(0) * TOGETHER + i
        kept = (row < left_sizes[d]) & (col < right_sizes[d])
        psi = jnp.where(kept, psi_ref[i], 0.0)
        parts = split3(psi)
        put(i, S_PSI, psi.T)
        for t in range(PAIRS // HELD):
            right = right_ref[t, i]
            product = dot3(parts, split3(right))
            put(i, S_RIGHT + 2 * t, right)
            put(i, S_PROD + 2 * t, product)
            put(i, S_TURN + 2 * t, product.T)


def send_kernel(source, rows, first, strip_ref, buf_ref, held_ref, sems):
    def copy(p, c):
        e = 4 * p + c
        return pltpu.make_async_copy(strip_ref.at[source[p, c]], held_ref.at[e], sems.at[e])

    places = [(p, c) for p in range(PAIRS) for c in range(4)]
    for p, c in places:
        @pl.when(rows[p, c] > 0)
        def _():
            copy(p, c).start()

    for p, c in places:
        @pl.when(rows[p, c] > 0)
        def _():
            copy(p, c).wait()
            begin = first[p, c]

            def four(i, inner):
                for k in range(4):
                    a = i * 4 + k
                    at = tile_rows(begin + a, ROWS_OUT)
                    tile = held_ref[4 * p + c, tile_at(a), :]
                    buf_ref[pl.ds(at, ROWS, stride=ROWS_OUT), :] = tile
                return inner

            lax.fori_loop(0, (rows[p, c] + 3) >> 2, four, 0)


def relay_kernel(idx, count, in_ref, out_ref):
    def slot(peer, carry):
        def some(i, inner):
            at = peer * ROWS_IN + i * ROWS
            for k in range(ROWS):
                out_ref[pl.ds(at + k, 1), :] = in_ref[pl.ds(idx[at + k], 1), :]
            return inner

        lax.fori_loop(0, (count[peer] + ROWS - 1) >> 3, some, 0)
        return carry

    lax.fori_loop(0, PEERS, slot, 0)


STREAM = MEMBERS * PIECE
SENT = PIECE + 1


def piece_at(place, core, chip):
    piece = ((place >> 2) ^ core) * 4 + ((place & 3) ^ chip)
    return pl.ds(pl.multiple_of(piece * PIECE, PIECE), PIECE)


def land_kernel(
    tbl, out_tbl, buf_ref, left_ref, keep_ref, send_ref, x_ref, y_ref, z_ref, sum_ref, stream_ref
):
    z_ref[...] = jnp.zeros_like(z_ref)

    def take(dst_ref, u, strip, before, rows):
        at = u * T_WIDTH
        start = tbl[at + T_START] + before
        begin = []
        for k in range(4):
            kind = (start + k) & 3
            rank = tbl[at + T_BASE + kind] + ((before + k) >> 2)
            begin.append((kind * (ROWS * ROWS_IN), rank))

        def four(i, carry):
            for k in range(4):
                first, rank = begin[k]
                row = first + jnp.minimum(rank + i, ROWS_IN - 1)
                dst_ref[u, tile_at(i * 4 + k), strip_at(strip)] = buf_ref[
                    pl.ds(row, ROWS, stride=ROWS_IN), :
                ]
            return carry

        lax.fori_loop(0, (rows + 3) >> 2, four, 0)

    def unpack(u, carry):
        at = u * T_WIDTH
        rows, nx, ny = tbl[at + T_ROWS], tbl[at + T_NX], tbl[at + T_NY]
        for strip in range(2):
            @pl.when(strip < nx)
            def _():
                take(x_ref, u, strip, strip * rows, rows)

            @pl.when(strip < ny)
            def _():
                take(y_ref, u, strip, (nx + strip) * rows, rows)

        return carry

    lax.fori_loop(0, PAIRS, unpack, 0)

    def blocks(rows):
        return (rows * ROWS + LANES - 1) >> 7

    def sector(d, carry):
        first, out_rows, strips, flip, m_blocks, n_blocks = (out_tbl[6 * d + i] for i in range(6))
        units = [d + t * HELD for t in range(PAIRS // HELD)]
        rows = [tbl[u * T_WIDTH + T_ROWS] for u in units]
        nx = [tbl[u * T_WIDTH + T_NX] for u in units]
        ny = [tbl[u * T_WIDTH + T_NY] for u in units]

        def masked(ref, t, height, width, count):
            row = lax.broadcasted_iota(jnp.int32, (height, width), 0)
            col = lax.broadcasted_iota(jnp.int32, (height, width), 1)
            kept = (row < rows[t] * ROWS) & (col < count * LANES)
            return jnp.where(kept, ref[units[t], :height, :width], 0.0)

        def turned(m, k, n):
            for t in range(2):
                z_ref[t, :m, :n] = dot3(
                    split3(left_ref[units[t], :m, :k]),
                    split3(masked(x_ref, t, n, k, nx[t])),
                    transposed=True,
                )

        inner_x = [jnp.where(nx[t] > 0, blocks(rows[t]), 0) for t in range(2)]
        variants(
            m_blocks, jnp.maximum(nx[0], nx[1]), jnp.maximum(inner_x[0], inner_x[1]), turned
        )

        def added(m, k, n):
            total = None
            for t in range(2):
                a = jnp.where(nx[t] > 0, z_ref[t, :m, :k], left_ref[units[t], :m, :k])
                part = dot3(split3(a), split3(masked(y_ref, t, k, n, ny[t])))
                part = part + jnp.where(ny[t] > 0, 0.0, z_ref[t, :m, :n])
                total = part if total is None else total + part

            @pl.when(flip == 0)
            def _():
                sum_ref[:m, :n] = total

            @pl.when(flip != 0)
            def _():
                sum_ref[:n, :m] = total.T

        inner_y = [jnp.where(ny[t] > 0, blocks(rows[t]), 1) for t in range(2)]
        variants(m_blocks, jnp.maximum(inner_y[0], inner_y[1]), n_blocks, added)

        for strip in range(2):
            @pl.when(strip < strips)
            def _():
                begin = first + strip * out_rows

                def four(i, inner):
                    at = jnp.minimum(begin + i * 4, STREAM)
                    for k in range(4):
                        stream_ref[at + k] = sum_ref[tile_at(i * 4 + k), strip_at(strip)]
                    return inner

                lax.fori_loop(0, (out_rows + 3) >> 2, four, 0)
        return carry

    lax.fori_loop(0, HELD, sector, 0)
    core, chip = out_tbl[O_CORE], out_tbl[O_CHIP]
    flag = jnp.full((ROWS, LANES), out_tbl[O_FLAG], jnp.int32).astype(jnp.float32)
    for place in range(4):
        into = pl.ds(place * SENT, PIECE)
        keep_ref[into] = stream_ref[piece_at(place, core, chip)]
        send_ref[into] = stream_ref[piece_at(place + 4, core, chip)]
        keep_ref[place * SENT + PIECE] = flag
        send_ref[place * SENT + PIECE] = flag


def spread_kernel(
    out_tbl, left_sizes, right_sizes, own_ref, other_ref, out_ref, stream_ref, block_ref, sems
):
    core, chip = out_tbl[O_CORE], out_tbl[O_CHIP]
    for place in range(4):
        part = pl.ds(place * SENT, PIECE)
        stream_ref[piece_at(place, core, chip)] = own_ref[part]
        stream_ref[piece_at(place + 4, core, chip)] = other_ref[part]

    row = lax.broadcasted_iota(jnp.int32, (ROWS, LANES), 0)
    col = lax.broadcasted_iota(jnp.int32, (ROWS, LANES), 1)
    def copy(d):
        return pltpu.make_async_copy(block_ref.at[d], out_ref.at[d], sems.at[d])

    def sector(d, carry):
        first, rows, strips, flip, high, wide = (out_tbl[6 * d + i] for i in range(6))
        height = jnp.where(flip > 0, right_sizes[d], left_sizes[d])
        width = jnp.where(flip > 0, left_sizes[d], right_sizes[d])
        block_ref[d] = jnp.zeros((BLK, BLK), jnp.float32)
        for strip in range(2):
            @pl.when(strip < strips)
            def _():
                begin = first + strip * rows
                col_ok = col + strip * LANES < width

                def four(i, inner):
                    at = jnp.minimum(begin + i * 4, STREAM)
                    for k in range(4):
                        a = i * 4 + k
                        kept = col_ok & (row + a * ROWS < height)
                        tile = jnp.where(kept, stream_ref[at + k], 0.0)
                        block_ref[d, tile_at(a), strip_at(strip)] = tile
                    return inner

                lax.fori_loop(0, (rows + 3) >> 2, four, 0)

        for n in (1, 2):
            for m in (1, 2):
                @pl.when((flip > 0) & (wide == n) & (high == m))
                def _():
                    rows, cols = n * LANES, m * LANES
                    turned = block_ref[d, :rows, :cols].T
                    if m < n:
                        block_ref[d, cols:rows, :cols] = jnp.zeros((rows - cols, cols), jnp.float32)
                    if n < m:
                        block_ref[d, :rows, rows:cols] = jnp.zeros((rows, cols - rows), jnp.float32)
                    block_ref[d, :cols, :rows] = turned

        copy(d).start()
        return carry

    def finish(d, carry):
        copy(d).wait()
        return carry

    lax.fori_loop(0, HELD, sector, 0)
    lax.fori_loop(0, HELD, finish, 0)


O_CORE, O_CHIP, O_FLAG = 6 * HELD, 6 * HELD + 1, 6 * HELD + 2

SMEM = pl.BlockSpec(memory_space=pltpu.SMEM)
VMEM = pl.BlockSpec(memory_space=pltpu.VMEM)
PARAMS = pltpu.CompilerParams(vmem_limit_bytes=VMEM_BYTES)
WIDEST = pltpu.CompilerParams(vmem_limit_bytes=WIDEST_BYTES)
WIDE = pltpu.CompilerParams(vmem_limit_bytes=WIDE_BYTES)


def floats(*shape):
    return jax.ShapeDtypeStruct(shape, jnp.float32)


def scratch(*shape):
    return pltpu.VMEM(shape, jnp.float32)


def carry_call(left_sizes, right_sizes, psi, right):
    return pl.pallas_call(
        carry_kernel,
        grid=(HELD // TOGETHER,),
        out_shape=floats(HELD, STRIPS, BLK, LANES),
        in_specs=[
            SMEM,
            SMEM,
            pl.BlockSpec((TOGETHER, BLK, BLK), lambda d: (d, 0, 0)),
            pl.BlockSpec((PAIRS // HELD, TOGETHER, BLK, BLK), lambda d: (0, d, 0, 0)),
        ],
        out_specs=pl.BlockSpec((TOGETHER, STRIPS, BLK, LANES), lambda d: (d, 0, 0, 0)),
        cost_estimate=pl.CostEstimate(
            flops=6 * PAIRS * BLK**3, bytes_accessed=24 * 2**20, transcendentals=0
        ),
        compiler_params=WIDE,
    )(left_sizes, right_sizes, psi, right)


def send_call(tables, strips):
    return pl.pallas_call(
        send_kernel,
        out_shape=floats(PEERS * ROWS_OUT, LANES),
        in_specs=[SMEM, SMEM, SMEM, pl.BlockSpec(memory_space=pl.ANY)],
        out_specs=VMEM,
        scratch_shapes=[
            scratch(4 * PAIRS, BLK, LANES),
            pltpu.SemaphoreType.DMA((4 * PAIRS,)),
        ],
        compiler_params=pltpu.CompilerParams(vmem_limit_bytes=SEND_BYTES),
    )(*tables, strips)


def relay_call(idx, count, received):
    return pl.pallas_call(
        relay_kernel,
        out_shape=floats(PEERS * ROWS_IN, LANES),
        in_specs=[SMEM, SMEM, VMEM],
        out_specs=VMEM,
        compiler_params=PARAMS,
    )(idx, count, received)


def land_call(tbl, out_tbl, received, left):
    return pl.pallas_call(
        land_kernel,
        out_shape=[floats(4 * SENT, ROWS, LANES)] * 2,
        in_specs=[SMEM, SMEM, VMEM, VMEM],
        out_specs=[VMEM, VMEM],
        scratch_shapes=[
            scratch(PAIRS, BLK, BLK),
            scratch(PAIRS, BLK, BLK),
            scratch(PAIRS // HELD, BLK, BLK),
            scratch(BLK, BLK),
            scratch(STREAM + ROWS, ROWS, LANES),
        ],
        compiler_params=PARAMS,
    )(tbl, out_tbl, received, left)


def spread_call(out_tbl, left_sizes, right_sizes, own, other):
    return pl.pallas_call(
        spread_kernel,
        out_shape=floats(HELD, BLK, BLK),
        in_specs=[SMEM, SMEM, SMEM, VMEM, VMEM],
        out_specs=pl.BlockSpec(memory_space=pl.ANY),
        scratch_shapes=[
            scratch(STREAM + ROWS, ROWS, LANES),
            scratch(HELD, BLK, BLK),
            pltpu.SemaphoreType.DMA((HELD,)),
        ],
        compiler_params=WIDEST,
    )(out_tbl, left_sizes, right_sizes, own, other)


def up(value, unit):
    return (value + (unit - 1)) >> (unit.bit_length() - 1)


def before(values, axis):
    n = values.shape[axis]
    moved = jnp.moveaxis(values, axis, -1)
    lower = np.arange(n)[:, None] > np.arange(n)[None, :]
    total = jnp.sum(jnp.where(lower, moved[..., None, :], 0), axis=-1)
    return jnp.moveaxis(total, -1, axis)


def make_tables(facts, me, core, chip):
    size_l, size_r = facts[:, 0], facts[:, 1]
    dest = facts[:, 2:].reshape(PEERS, PAIRS)

    ls = jnp.concatenate([size_l, size_l], axis=1)
    rs = jnp.concatenate([size_r, size_r], axis=1)
    to_dev = dest >> 3
    hit_dev = to_dev[:, :, None] == np.arange(PEERS, dtype=np.int32)[None, None, :]
    sector = np.arange(PEERS * HELD, dtype=np.int32)[:, None]
    rd = jnp.sum(
        jnp.where(dest.reshape(1, -1) == sector, size_r.reshape(-1)[:, None], 0), axis=0
    ).reshape(PEERS, PAIRS)
    nl, nr = up(ls, LANES), up(rd, LANES)
    cost_c = up(ls, ROWS) * nr
    cost_ct = up(rd, ROWS) * nl
    cost_f = up(rs, ROWS) * (nl + nr)
    is_f = (cost_f < cost_c) & (cost_f < cost_ct)
    is_ct = ~is_f & (cost_ct < cost_c)
    rows = up(jnp.where(is_f, rs, jnp.where(is_ct, rd, ls)), ROWS)
    nx = jnp.where(is_f | is_ct, nl, 0)
    ny = jnp.where(is_ct, 0, nr)
    tiles = rows * (nx + ny)
    start = before(tiles, 1)
    total = jnp.sum(tiles, axis=1)

    kinds = np.arange(4, dtype=np.int32)[:, None, None]
    lag = (kinds - start) & 3
    share = (tiles + 3 - lag) >> 2
    first_row = (start + lag) >> 2
    onto = jnp.sum(jnp.where(hit_dev[None], share[..., None], 0), axis=2)
    base = before(onto, 1)
    filled = jnp.sum(onto, axis=1)

    high, wide = up(size_l, LANES), up(size_r, LANES)
    flip = (up(size_r, ROWS) * high < up(size_l, ROWS) * wide).astype(jnp.int32)
    out_rows = up(jnp.where(flip > 0, size_r, size_l), ROWS)
    out_strips = jnp.where(flip > 0, high, wide)
    out_tiles = out_rows * out_strips
    out_first = before(out_tiles, 1)
    spilled = (
        jnp.any(total > 4 * (ROWS_OUT - 1))
        | jnp.any(filled > ROWS_IN)
        | jnp.any(jnp.sum(out_tiles, axis=1) > MEMBERS * PIECE)
    )

    def own(values, axis=0):
        return lax.dynamic_index_in_dim(values, me, axis, keepdims=False)

    pair = np.arange(PAIRS, dtype=np.int32)[:, None]
    place = np.arange(4, dtype=np.int32)[None, :]
    own_nx, own_ny, own_rows = own(nx)[:, None], own(ny)[:, None], own(rows)[:, None]
    both = (own_nx > 0) & (own_ny > 0)
    term, held = pair // HELD, pair % HELD
    source = jnp.where(
        place < 2,
        jnp.where(both, S_PSI, S_TURN + 2 * term),
        jnp.where(both, S_RIGHT, S_PROD) + 2 * term,
    )
    source = held * STRIPS + source + place % 2
    used = jnp.where(place < 2, place < own_nx, place - 2 < own_ny)
    index = jnp.where(place < 2, place, own_nx + place - 2)
    send_tbl = (
        source,
        jnp.where(used, own_rows, 0),
        own(start)[:, None] + index * own_rows,
    )

    kind = me >> 3
    onto_k = lax.dynamic_index_in_dim(onto, kind, 0, keepdims=False)
    base_k = lax.dynamic_index_in_dim(base, kind, 0, keepdims=False)
    first_k = lax.dynamic_index_in_dim(first_row, kind, 0, keepdims=False)
    filled_k = lax.dynamic_index_in_dim(filled, kind, 0, keepdims=False)
    first_to = jnp.sum(jnp.where(hit_dev, first_k[:, :, None], 0), axis=1)
    rank = np.arange(ROWS_IN, dtype=np.int32)[None, None, :]
    here = (rank >= base_k[:, :, None]) & (rank < (base_k + onto_k)[:, :, None])
    origin = np.arange(PEERS, dtype=np.int32)[:, None] * ROWS_OUT + first_to - base_k
    relay_idx = jnp.sum(jnp.where(here, origin[:, :, None] + rank, 0), axis=0)
    relay_idx = jnp.clip(relay_idx, 0, PEERS * ROWS_OUT - 1).reshape(-1)
    relay_count = jnp.minimum(filled_k, ROWS_IN)

    unit = np.arange(PAIRS, dtype=np.int32)[:, None, None]
    reach = (dest[None] == me * HELD + unit % HELD) & (
        (np.arange(PAIRS, dtype=np.int32) // HELD)[None, None, :] == unit // HELD
    )

    def reached(values):
        return jnp.sum(jnp.where(reach, values[None], 0), axis=(1, 2))

    base_me = lax.dynamic_index_in_dim(base, me, 2, keepdims=False)
    land_tbl = jnp.stack(
        [reached(start), reached(rows), reached(nx), reached(ny), reached(ls), reached(rs)]
        + [reached(jnp.broadcast_to(base_me[g][:, None], (PEERS, PAIRS))) for g in range(4)],
        axis=1,
    ).reshape(-1)

    out_tbl = jnp.concatenate(
        [
            jnp.stack(
                [own(v) for v in (out_first, out_rows, out_strips, flip, high, wide)], axis=1
            ).reshape(-1),
            jnp.stack([core, chip, spilled.astype(jnp.int32)]).astype(jnp.int32),
        ]
    )
    return send_tbl, relay_idx, relay_count, land_tbl, out_tbl


def per_device(psi_blocks, left_env, right_env, left_sizes, right_sizes, dest_sector):
    me = lax.axis_index("sec")
    member = lax.axis_index("term")
    core, chip = member & 1, member >> 1
    strips = carry_call(left_sizes, right_sizes, psi_blocks, right_env)
    strips = strips.reshape(HELD * STRIPS, BLK, LANES)
    mine = jnp.concatenate([left_sizes[None], right_sizes[None], dest_sector])
    mine = jnp.broadcast_to(mine[None], (PEERS, 4, HELD))
    facts = lax.all_to_all(mine, "sec", 0, 0, tiled=True)
    tables = make_tables(facts, me, core, chip)
    send_tbl, relay_idx, relay_count, land_tbl, out_tbl = tables

    sent = send_call(send_tbl, strips)
    hop = lax.all_to_all(sent.reshape(PEERS, ROWS_OUT, LANES), "sec", 0, 0, tiled=True)
    passed = relay_call(relay_idx, relay_count, hop.reshape(PEERS * ROWS_OUT, LANES))
    hop = lax.all_to_all(passed.reshape(PEERS, ROWS_IN, LANES), "sec", 0, 0, tiled=True)
    keep, give = land_call(
        land_tbl,
        out_tbl,
        hop.reshape(PEERS * ROWS_IN, LANES),
        left_env.reshape(PAIRS, BLK, BLK),
    )

    def swap(values, bits):
        return lax.ppermute(values, "term", [(i, i ^ bits) for i in range(MEMBERS)])

    half = (keep + swap(give, 1)).reshape(4, SENT, ROWS, LANES)
    piece = half[0] + swap(half[1], 2) + swap(half[2], 4) + swap(half[3], 6)
    whole = jnp.concatenate([piece, swap(piece, 2), swap(piece, 4), swap(piece, 6)])
    other = swap(whole, 1)

    return lax.cond(
        piece[PIECE, 0, 0] > 0.5,
        lambda: dense_program(
            psi_blocks, left_env, right_env, left_sizes, right_sizes, dest_sector
        ),
        lambda: spread_call(out_tbl, left_sizes, right_sizes, whole, other),
    )


def solution(mesh):
    in_specs = (
        P("sec", None, None),
        P("term", "sec", None, None),
        P("term", "sec", None, None),
        P("sec"),
        P("sec"),
        P("term", "sec"),
    )
    out_specs = P("sec", None, None)
    return jax.shard_map(
        per_device, mesh=mesh, in_specs=in_specs, out_specs=out_specs, check_vma=False
    )
```

```python
import functools
import jax
import jax.numpy as jnp
import numpy as np
from jax import lax
from jax.experimental import pallas as pl
from jax.experimental.pallas import tpu as pltpu
from jax.sharding import PartitionSpec as P

BLK = 256
LANES = 128
ROWS = 8
PEERS = 32
MEMBERS = 8
HELD = 8
PAIRS = 16
SLOT_ROWS = (64, 104)
PIECE = 24
VMEM_BYTES = 24 * 1024 * 1024
WIDE_BYTES = 56 * 1024 * 1024
WIDEST_BYTES = 62 * 1024 * 1024
SEND_BYTES = 50 * 1024 * 1024


def sector_mask(left_sizes, right_sizes, block_size):
    positions = jnp.arange(block_size, dtype=jnp.int32)
    row_ok = positions[None, :, None] < left_sizes[:, None, None]
    col_ok = positions[None, None, :] < right_sizes[:, None, None]
    return (row_ok & col_ok).astype(jnp.float32)


def pack_blocks(outgoing, targets, term_ids, sector_local, capacity, slot_count):
    target_device = targets // sector_local
    target_place = targets % sector_local
    count_out = targets.shape[0]
    order_index = jnp.arange(count_out, dtype=jnp.int32)
    same_device = target_device[:, None] == target_device[None, :]
    earlier = order_index[None, :] < order_index[:, None]
    peer_rank = jnp.sum((same_device & earlier).astype(jnp.int32), axis=1)
    send_slot = target_device * capacity + peer_rank
    chosen = jnp.arange(slot_count, dtype=jnp.int32)[:, None] == send_slot[None, :]
    slot_source = jnp.sum(jnp.where(chosen, order_index[None, :], 0), axis=1)
    filled = jnp.any(chosen, axis=1)
    buffer = jnp.where(filled[:, None, None], outgoing[slot_source], 0.0)
    left_code = term_ids * sector_local + target_place
    meta_codes = jnp.where(filled, left_code[slot_source], -1)
    return (buffer, meta_codes)


def apply_left(received, meta_codes, flat_left, sector_local, live_count):
    slot_count = meta_codes.shape[0]
    is_valid = meta_codes >= 0
    live_rank = jnp.cumsum(is_valid.astype(jnp.int32)) - 1
    wanted = jnp.arange(live_count, dtype=jnp.int32)
    picked = (live_rank[None, :] == wanted[:, None]) & is_valid[None, :]
    slot_index = jnp.arange(slot_count, dtype=jnp.int32)
    source_slot = jnp.sum(jnp.where(picked, slot_index[None, :], 0), axis=1)
    compact_blocks = received[source_slot]
    compact_codes = meta_codes[source_slot]
    chosen_left = flat_left[compact_codes]
    landed = jnp.einsum(
        "pab,pbc->pac", chosen_left, compact_blocks, precision=lax.Precision.HIGHEST
    )
    target_place = compact_codes % sector_local
    onehot_place = target_place[:, None] == jnp.arange(sector_local, dtype=jnp.int32)[None, :]
    return jnp.einsum(
        "pk,pac->kac", onehot_place.astype(jnp.float32), landed, precision=lax.Precision.HIGHEST
    )


def dense_program(psi_blocks, left_env, right_env, left_sizes, right_sizes, dest_sector):
    term_local = left_env.shape[0]
    sector_local = left_env.shape[1]
    block_size = left_env.shape[2]
    peers = lax.axis_size("sec")
    capacity = (term_local * sector_local + peers - 1) // peers
    slot_count = peers * capacity
    valid_mask = sector_mask(left_sizes, right_sizes, block_size)
    masked_psi = psi_blocks * valid_mask
    carried = jnp.einsum("sab,tsbc->tsac", masked_psi, right_env, precision=lax.Precision.HIGHEST)
    flat_left = left_env.reshape(term_local * sector_local, block_size, block_size)
    term_ids = jnp.repeat(jnp.arange(term_local, dtype=jnp.int32), sector_local)
    buffer, meta_codes = pack_blocks(
        carried.reshape(term_local * sector_local, block_size, block_size),
        dest_sector.reshape(term_local * sector_local),
        term_ids,
        sector_local,
        capacity,
        slot_count,
    )
    received, codes_in = (
        lax.all_to_all(buffer, "sec", split_axis=0, concat_axis=0, tiled=True),
        lax.all_to_all(meta_codes, "sec", split_axis=0, concat_axis=0, tiled=True),
    )
    partial_sum = apply_left(received, codes_in, flat_left, sector_local, term_local * sector_local)
    total = lax.psum(partial_sum, "term")
    return total * valid_mask


def split3(a):
    hi = a.astype(jnp.bfloat16)
    lo = (a - hi.astype(jnp.float32)).astype(jnp.bfloat16)
    return hi, lo


def dot3(a, b, transposed=False):
    dims = (((1,), (1 if transposed else 0,)), ((), ()))
    mul = functools.partial(
        lax.dot_general, dimension_numbers=dims, preferred_element_type=jnp.float32
    )
    return mul(a[0], b[0]) + (mul(a[0], b[1]) + mul(a[1], b[0]))


T_START, T_ROWS, T_NX, T_NY, T_LEFT, T_RIGHT, T_BASE = 0, 1, 2, 3, 4, 5, 6
T_WIDTH = 10


def tile_rows(stream, rows):
    return (stream & 3) * (ROWS * rows) + jnp.minimum(stream >> 2, rows - 1)


def tile_at(a):
    return pl.ds(pl.multiple_of(a * ROWS, ROWS), ROWS)


def strip_at(strip):
    return pl.ds(strip * LANES, LANES)


def block_at(i):
    return pl.ds(pl.multiple_of(i * LANES, LANES), LANES)


def variants(m_blocks, k_blocks, n_blocks, body):
    code = m_blocks * 4 + k_blocks * 2 + n_blocks - 7
    for m in (1, 2):
        for k in (1, 2):
            for n in (1, 2):
                @pl.when((code == m * 4 + k * 2 + n - 7) & (k_blocks > 0))
                def _():
                    body(m * LANES, k * LANES, n * LANES)


S_PSI, S_PROD, S_TURN, S_RIGHT, STRIPS = 0, 2, 6, 10, 14
TOGETHER = 2


def carry_kernel(left_sizes, right_sizes, psi_ref, right_ref, strip_ref):
    row = lax.broadcasted_iota(jnp.int32, (BLK, BLK), 0)
    col = lax.broadcasted_iota(jnp.int32, (BLK, BLK), 1)

    def put(i, first, block):
        for strip in range(2):
            strip_ref[i, first + strip] = block[:, strip * LANES : (strip + 1) * LANES]

    for i in range(TOGETHER):
        d = pl.program_id(0) * TOGETHER + i
        kept = (row < left_sizes[d]) & (col < right_sizes[d])
        psi = jnp.where(kept, psi_ref[i], 0.0)
        parts = split3(psi)
        put(i, S_PSI, psi.T)
        for t in range(PAIRS // HELD):
            right = right_ref[t, i]
            product = dot3(parts, split3(right))
            put(i, S_RIGHT + 2 * t, right)
            put(i, S_PROD + 2 * t, product)
            put(i, S_TURN + 2 * t, product.T)


def send_kernel(slot, source, rows, first, strip_ref, buf_ref, held_ref, sems):
    def copy(p, c):
        e = 4 * p + c
        return pltpu.make_async_copy(strip_ref.at[source[p, c]], held_ref.at[e], sems.at[e])

    places = [(p, c) for p in range(PAIRS) for c in range(4)]
    for p, c in places:
        @pl.when(rows[p, c] > 0)
        def _():
            copy(p, c).start()

    for p, c in places:
        @pl.when(rows[p, c] > 0)
        def _():
            copy(p, c).wait()
            begin = first[p, c]

            def four(i, inner):
                for k in range(4):
                    a = i * 4 + k
                    at = tile_rows(begin + a, slot)
                    tile = held_ref[4 * p + c, tile_at(a), :]
                    buf_ref[pl.ds(at, ROWS, stride=slot), :] = tile
                return inner

            lax.fori_loop(0, (rows[p, c] + 3) >> 2, four, 0)


def relay_kernel(slot, idx, count, in_ref, out_ref):
    def fill(peer, carry):
        def some(i, inner):
            at = peer * slot + i * ROWS
            for k in range(ROWS):
                out_ref[pl.ds(at + k, 1), :] = in_ref[pl.ds(idx[at + k], 1), :]
            return inner

        lax.fori_loop(0, (count[peer] + ROWS - 1) >> 3, some, 0)
        return carry

    lax.fori_loop(0, PEERS, fill, 0)


STREAM = MEMBERS * PIECE
SENT = PIECE + 1


def piece_at(place, core, chip):
    piece = ((place >> 2) ^ core) * 4 + ((place & 3) ^ chip)
    return pl.ds(pl.multiple_of(piece * PIECE, PIECE), PIECE)


def land_kernel(
    slot, tbl, out_tbl, buf_ref, left_ref, keep_ref, send_ref, x_ref, y_ref, z_ref, sum_ref, stream_ref
):
    z_ref[...] = jnp.zeros_like(z_ref)

    def take(dst_ref, u, strip, before, rows):
        at = u * T_WIDTH
        start = tbl[at + T_START] + before
        begin = []
        for k in range(4):
            kind = (start + k) & 3
            rank = tbl[at + T_BASE + kind] + ((before + k) >> 2)
            begin.append((kind * (ROWS * slot), rank))

        def four(i, carry):
            for k in range(4):
                first, rank = begin[k]
                row = first + jnp.minimum(rank + i, slot - 1)
                dst_ref[u, tile_at(i * 4 + k), strip_at(strip)] = buf_ref[
                    pl.ds(row, ROWS, stride=slot), :
                ]
            return carry

        lax.fori_loop(0, (rows + 3) >> 2, four, 0)

    def unpack(u, carry):
        at = u * T_WIDTH
        rows, nx, ny = tbl[at + T_ROWS], tbl[at + T_NX], tbl[at + T_NY]
        for strip in range(2):
            @pl.when(strip < nx)
            def _():
                take(x_ref, u, strip, strip * rows, rows)

            @pl.when(strip < ny)
            def _():
                take(y_ref, u, strip, (nx + strip) * rows, rows)

        return carry

    lax.fori_loop(0, PAIRS, unpack, 0)

    def blocks(rows):
        return (rows * ROWS + LANES - 1) >> 7

    def sector(d, carry):
        first, out_rows, strips, flip, m_blocks, n_blocks = (out_tbl[6 * d + i] for i in range(6))
        units = [d + t * HELD for t in range(PAIRS // HELD)]
        rows = [tbl[u * T_WIDTH + T_ROWS] for u in units]
        nx = [tbl[u * T_WIDTH + T_NX] for u in units]
        ny = [tbl[u * T_WIDTH + T_NY] for u in units]

        def masked(ref, t, height, width, count):
            row = lax.broadcasted_iota(jnp.int32, (height, width), 0)
            col = lax.broadcasted_iota(jnp.int32, (height, width), 1)
            kept = (row < rows[t] * ROWS) & (col < count * LANES)
            return jnp.where(kept, ref[units[t], :height, :width], 0.0)

        def turned(m, k, n):
            for t in range(2):
                z_ref[t, :m, :n] = dot3(
                    split3(left_ref[units[t], :m, :k]),
                    split3(masked(x_ref, t, n, k, nx[t])),
                    transposed=True,
                )

        inner_x = [jnp.where(nx[t] > 0, blocks(rows[t]), 0) for t in range(2)]
        variants(
            m_blocks, jnp.maximum(nx[0], nx[1]), jnp.maximum(inner_x[0], inner_x[1]), turned
        )

        def added(m, k, n):
            total = None
            for t in range(2):
                a = jnp.where(nx[t] > 0, z_ref[t, :m, :k], left_ref[units[t], :m, :k])
                part = dot3(split3(a), split3(masked(y_ref, t, k, n, ny[t])))
                part = part + jnp.where(ny[t] > 0, 0.0, z_ref[t, :m, :n])
                total = part if total is None else total + part

            @pl.when(flip == 0)
            def _():
                sum_ref[:m, :n] = total

            @pl.when(flip != 0)
            def _():
                sum_ref[:n, :m] = total.T

        inner_y = [jnp.where(ny[t] > 0, blocks(rows[t]), 1) for t in range(2)]
        variants(m_blocks, jnp.maximum(inner_y[0], inner_y[1]), n_blocks, added)

        for strip in range(2):
            @pl.when(strip < strips)
            def _():
                begin = first + strip * out_rows

                def four(i, inner):
                    at = jnp.minimum(begin + i * 4, STREAM)
                    for k in range(4):
                        stream_ref[at + k] = sum_ref[tile_at(i * 4 + k), strip_at(strip)]
                    return inner

                lax.fori_loop(0, (out_rows + 3) >> 2, four, 0)
        return carry

    lax.fori_loop(0, HELD, sector, 0)
    core, chip = out_tbl[O_CORE], out_tbl[O_CHIP]
    flag = jnp.full((ROWS, LANES), out_tbl[O_FLAG], jnp.int32).astype(jnp.float32)
    for place in range(4):
        into = pl.ds(place * SENT, PIECE)
        keep_ref[into] = stream_ref[piece_at(place, core, chip)]
        send_ref[into] = stream_ref[piece_at(place + 4, core, chip)]
        keep_ref[place * SENT + PIECE] = flag
        send_ref[place * SENT + PIECE] = flag


def spread_kernel(
    out_tbl, left_sizes, right_sizes, own_ref, other_ref, out_ref, stream_ref, block_ref, sems
):
    core, chip = out_tbl[O_CORE], out_tbl[O_CHIP]
    for place in range(4):
        part = pl.ds(place * SENT, PIECE)
        stream_ref[piece_at(place, core, chip)] = own_ref[part]
        stream_ref[piece_at(place + 4, core, chip)] = other_ref[part]

    row = lax.broadcasted_iota(jnp.int32, (ROWS, LANES), 0)
    col = lax.broadcasted_iota(jnp.int32, (ROWS, LANES), 1)
    def copy(d):
        return pltpu.make_async_copy(block_ref.at[d], out_ref.at[d], sems.at[d])

    def sector(d, carry):
        first, rows, strips, flip, high, wide = (out_tbl[6 * d + i] for i in range(6))
        height = jnp.where(flip > 0, right_sizes[d], left_sizes[d])
        width = jnp.where(flip > 0, left_sizes[d], right_sizes[d])
        block_ref[d] = jnp.zeros((BLK, BLK), jnp.float32)
        for strip in range(2):
            @pl.when(strip < strips)
            def _():
                begin = first + strip * rows
                col_ok = col + strip * LANES < width

                def four(i, inner):
                    at = jnp.minimum(begin + i * 4, STREAM)
                    for k in range(4):
                        a = i * 4 + k
                        kept = col_ok & (row + a * ROWS < height)
                        tile = jnp.where(kept, stream_ref[at + k], 0.0)
                        block_ref[d, tile_at(a), strip_at(strip)] = tile
                    return inner

                lax.fori_loop(0, (rows + 3) >> 2, four, 0)

        for n in (1, 2):
            for m in (1, 2):
                @pl.when((flip > 0) & (wide == n) & (high == m))
                def _():
                    rows, cols = n * LANES, m * LANES
                    turned = block_ref[d, :rows, :cols].T
                    if m < n:
                        block_ref[d, cols:rows, :cols] = jnp.zeros((rows - cols, cols), jnp.float32)
                    if n < m:
                        block_ref[d, :rows, rows:cols] = jnp.zeros((rows, cols - rows), jnp.float32)
                    block_ref[d, :cols, :rows] = turned

        copy(d).start()
        return carry

    def finish(d, carry):
        copy(d).wait()
        return carry

    lax.fori_loop(0, HELD, sector, 0)
    lax.fori_loop(0, HELD, finish, 0)


O_CORE, O_CHIP, O_FLAG = 6 * HELD, 6 * HELD + 1, 6 * HELD + 2

SMEM = pl.BlockSpec(memory_space=pltpu.SMEM)
VMEM = pl.BlockSpec(memory_space=pltpu.VMEM)
PARAMS = pltpu.CompilerParams(vmem_limit_bytes=VMEM_BYTES)
WIDEST = pltpu.CompilerParams(vmem_limit_bytes=WIDEST_BYTES)
WIDE = pltpu.CompilerParams(vmem_limit_bytes=WIDE_BYTES)


def floats(*shape):
    return jax.ShapeDtypeStruct(shape, jnp.float32)


def scratch(*shape):
    return pltpu.VMEM(shape, jnp.float32)


def carry_call(left_sizes, right_sizes, psi, right):
    return pl.pallas_call(
        carry_kernel,
        grid=(HELD // TOGETHER,),
        out_shape=floats(HELD, STRIPS, BLK, LANES),
        in_specs=[
            SMEM,
            SMEM,
            pl.BlockSpec((TOGETHER, BLK, BLK), lambda d: (d, 0, 0)),
            pl.BlockSpec((PAIRS // HELD, TOGETHER, BLK, BLK), lambda d: (0, d, 0, 0)),
        ],
        out_specs=pl.BlockSpec((TOGETHER, STRIPS, BLK, LANES), lambda d: (d, 0, 0, 0)),
        cost_estimate=pl.CostEstimate(
            flops=6 * PAIRS * BLK**3, bytes_accessed=24 * 2**20, transcendentals=0
        ),
        compiler_params=WIDE,
    )(left_sizes, right_sizes, psi, right)


def send_call(slot, tables, strips):
    return pl.pallas_call(
        functools.partial(send_kernel, slot),
        out_shape=floats(PEERS * slot, LANES),
        in_specs=[SMEM, SMEM, SMEM, pl.BlockSpec(memory_space=pl.ANY)],
        out_specs=VMEM,
        scratch_shapes=[
            scratch(4 * PAIRS, BLK, LANES),
            pltpu.SemaphoreType.DMA((4 * PAIRS,)),
        ],
        compiler_params=pltpu.CompilerParams(vmem_limit_bytes=SEND_BYTES),
    )(*tables, strips)


def relay_call(slot, idx, count, received):
    return pl.pallas_call(
        functools.partial(relay_kernel, slot),
        out_shape=floats(PEERS * slot, LANES),
        in_specs=[SMEM, SMEM, VMEM],
        out_specs=VMEM,
        compiler_params=PARAMS,
    )(idx, count, received)


def land_call(slot, tbl, out_tbl, received, left):
    return pl.pallas_call(
        functools.partial(land_kernel, slot),
        out_shape=[floats(4 * SENT, ROWS, LANES)] * 2,
        in_specs=[SMEM, SMEM, VMEM, VMEM],
        out_specs=[VMEM, VMEM],
        scratch_shapes=[
            scratch(PAIRS, BLK, BLK),
            scratch(PAIRS, BLK, BLK),
            scratch(PAIRS // HELD, BLK, BLK),
            scratch(BLK, BLK),
            scratch(STREAM + ROWS, ROWS, LANES),
        ],
        compiler_params=PARAMS,
    )(tbl, out_tbl, received, left)


def spread_call(out_tbl, left_sizes, right_sizes, own, other):
    return pl.pallas_call(
        spread_kernel,
        out_shape=floats(HELD, BLK, BLK),
        in_specs=[SMEM, SMEM, SMEM, VMEM, VMEM],
        out_specs=pl.BlockSpec(memory_space=pl.ANY),
        scratch_shapes=[
            scratch(STREAM + ROWS, ROWS, LANES),
            scratch(HELD, BLK, BLK),
            pltpu.SemaphoreType.DMA((HELD,)),
        ],
        compiler_params=WIDEST,
    )(out_tbl, left_sizes, right_sizes, own, other)


def up(value, unit):
    return (value + (unit - 1)) >> (unit.bit_length() - 1)


def before(values, axis):
    n = values.shape[axis]
    moved = jnp.moveaxis(values, axis, -1)
    lower = np.arange(n)[:, None] > np.arange(n)[None, :]
    total = jnp.sum(jnp.where(lower, moved[..., None, :], 0), axis=-1)
    return jnp.moveaxis(total, -1, axis)


def make_tables(facts, me, core, chip):
    size_l, size_r = facts[:, 0], facts[:, 1]
    dest = facts[:, 2:].reshape(PEERS, PAIRS)

    ls = jnp.concatenate([size_l, size_l], axis=1)
    rs = jnp.concatenate([size_r, size_r], axis=1)
    to_dev = dest >> 3
    hit_dev = to_dev[:, :, None] == np.arange(PEERS, dtype=np.int32)[None, None, :]
    sector = np.arange(PEERS * HELD, dtype=np.int32)[:, None]
    rd = jnp.sum(
        jnp.where(dest.reshape(1, -1) == sector, size_r.reshape(-1)[:, None], 0), axis=0
    ).reshape(PEERS, PAIRS)
    nl, nr = up(ls, LANES), up(rd, LANES)
    cost_c = up(ls, ROWS) * nr
    cost_ct = up(rd, ROWS) * nl
    cost_f = up(rs, ROWS) * (nl + nr)
    is_f = (cost_f < cost_c) & (cost_f < cost_ct)
    is_ct = ~is_f & (cost_ct < cost_c)
    rows = up(jnp.where(is_f, rs, jnp.where(is_ct, rd, ls)), ROWS)
    nx = jnp.where(is_f | is_ct, nl, 0)
    ny = jnp.where(is_ct, 0, nr)
    tiles = rows * (nx + ny)
    start = before(tiles, 1)
    total = jnp.sum(tiles, axis=1)

    kinds = np.arange(4, dtype=np.int32)[:, None, None]
    lag = (kinds - start) & 3
    share = (tiles + 3 - lag) >> 2
    first_row = (start + lag) >> 2
    onto = jnp.sum(jnp.where(hit_dev[None], share[..., None], 0), axis=2)
    base = before(onto, 1)
    filled = jnp.sum(onto, axis=1)

    high, wide = up(size_l, LANES), up(size_r, LANES)
    flip = (up(size_r, ROWS) * high < up(size_l, ROWS) * wide).astype(jnp.int32)
    out_rows = up(jnp.where(flip > 0, size_r, size_l), ROWS)
    out_strips = jnp.where(flip > 0, high, wide)
    out_tiles = out_rows * out_strips
    out_first = before(out_tiles, 1)
    crowded = jnp.any(jnp.sum(out_tiles, axis=1) > MEMBERS * PIECE)

    def spilled(slot):
        return jnp.any(total > 4 * (slot - 1)) | jnp.any(filled > slot) | crowded

    def own(values, axis=0):
        return lax.dynamic_index_in_dim(values, me, axis, keepdims=False)

    pair = np.arange(PAIRS, dtype=np.int32)[:, None]
    place = np.arange(4, dtype=np.int32)[None, :]
    own_nx, own_ny, own_rows = own(nx)[:, None], own(ny)[:, None], own(rows)[:, None]
    both = (own_nx > 0) & (own_ny > 0)
    term, held = pair // HELD, pair % HELD
    source = jnp.where(
        place < 2,
        jnp.where(both, S_PSI, S_TURN + 2 * term),
        jnp.where(both, S_RIGHT, S_PROD) + 2 * term,
    )
    source = held * STRIPS + source + place % 2
    used = jnp.where(place < 2, place < own_nx, place - 2 < own_ny)
    index = jnp.where(place < 2, place, own_nx + place - 2)
    send_tbl = (
        source,
        jnp.where(used, own_rows, 0),
        own(start)[:, None] + index * own_rows,
    )

    kind = me >> 3
    onto_k = lax.dynamic_index_in_dim(onto, kind, 0, keepdims=False)
    base_k = lax.dynamic_index_in_dim(base, kind, 0, keepdims=False)
    first_k = lax.dynamic_index_in_dim(first_row, kind, 0, keepdims=False)
    filled_k = lax.dynamic_index_in_dim(filled, kind, 0, keepdims=False)
    first_to = jnp.sum(jnp.where(hit_dev, first_k[:, :, None], 0), axis=1)

    def relay_tbl(slot):
        rank = np.arange(slot, dtype=np.int32)[None, None, :]
        here = (rank >= base_k[:, :, None]) & (rank < (base_k + onto_k)[:, :, None])
        origin = np.arange(PEERS, dtype=np.int32)[:, None] * slot + first_to - base_k
        idx = jnp.sum(jnp.where(here, origin[:, :, None] + rank, 0), axis=0)
        return jnp.clip(idx, 0, PEERS * slot - 1).reshape(-1), jnp.minimum(filled_k, slot)

    unit = np.arange(PAIRS, dtype=np.int32)[:, None, None]
    reach = (dest[None] == me * HELD + unit % HELD) & (
        (np.arange(PAIRS, dtype=np.int32) // HELD)[None, None, :] == unit // HELD
    )

    def reached(values):
        return jnp.sum(jnp.where(reach, values[None], 0), axis=(1, 2))

    base_me = lax.dynamic_index_in_dim(base, me, 2, keepdims=False)
    land_tbl = jnp.stack(
        [reached(start), reached(rows), reached(nx), reached(ny), reached(ls), reached(rs)]
        + [reached(jnp.broadcast_to(base_me[g][:, None], (PEERS, PAIRS))) for g in range(4)],
        axis=1,
    ).reshape(-1)

    def out_tbl(slot):
        lines = [own(v) for v in (out_first, out_rows, out_strips, flip, high, wide)]
        last = jnp.stack([core, chip, spilled(slot).astype(jnp.int32)]).astype(jnp.int32)
        return jnp.concatenate([jnp.stack(lines, axis=1).reshape(-1), last])

    return send_tbl, relay_tbl, land_tbl, out_tbl


def per_device(psi_blocks, left_env, right_env, left_sizes, right_sizes, dest_sector):
    me = lax.axis_index("sec")
    member = lax.axis_index("term")
    core, chip = member & 1, member >> 1
    strips = carry_call(left_sizes, right_sizes, psi_blocks, right_env)
    strips = strips.reshape(HELD * STRIPS, BLK, LANES)
    mine = jnp.concatenate([left_sizes[None], right_sizes[None], dest_sector])
    mine = jnp.broadcast_to(mine[None], (PEERS, 4, HELD))
    facts = lax.all_to_all(mine, "sec", 0, 0, tiled=True)
    tables = make_tables(facts, me, core, chip)
    send_tbl, relay_tbl, land_tbl, out_tbl = tables

    def swap(values, bits):
        return lax.ppermute(values, "term", [(i, i ^ bits) for i in range(MEMBERS)])

    def packed_program(slot, otherwise):
        def exchange(rows):
            there = lax.all_to_all(rows.reshape(PEERS, slot, LANES), "sec", 0, 0, tiled=True)
            return there.reshape(PEERS * slot, LANES)

        arrived = exchange(send_call(slot, send_tbl, strips))
        idx, count = relay_tbl(slot)
        arrived = exchange(relay_call(slot, idx, count, arrived))
        left = left_env.reshape(PAIRS, BLK, BLK)
        lines = out_tbl(slot)
        keep, give = land_call(slot, land_tbl, lines, arrived, left)
        half = (keep + swap(give, 1)).reshape(4, SENT, ROWS, LANES)
        piece = half[0] + swap(half[1], 2) + swap(half[2], 4) + swap(half[3], 6)
        whole = jnp.concatenate([piece, swap(piece, 2), swap(piece, 4), swap(piece, 6)])
        other = swap(whole, 1)
        return lax.cond(
            piece[PIECE, 0, 0] > 0.5,
            otherwise,
            lambda: spread_call(lines, left_sizes, right_sizes, whole, other),
        )

    def dense():
        return dense_program(
            psi_blocks, left_env, right_env, left_sizes, right_sizes, dest_sector
        )

    usual, tall = SLOT_ROWS
    return packed_program(usual, lambda: packed_program(tall, dense))


def solution(mesh):
    in_specs = (
        P("sec", None, None),
        P("term", "sec", None, None),
        P("term", "sec", None, None),
        P("sec"),
        P("sec"),
        P("term", "sec"),
    )
    out_specs = P("sec", None, None)
    return jax.shard_map(
        per_device, mesh=mesh, in_specs=in_specs, out_specs=out_specs, check_vma=False
    )
```

```python
import functools
import jax
import jax.numpy as jnp
import numpy as np
from jax import lax
from jax.experimental import pallas as pl
from jax.experimental.pallas import tpu as pltpu
from jax.sharding import PartitionSpec as P

BLK = 256
LANES = 128
ROWS = 8
PEERS = 32
MEMBERS = 8
HELD = 8
PAIRS = 16
SLOT_ROWS = (64, 104)
PIECE = 24
VMEM_BYTES = 24 * 1024 * 1024
WIDE_BYTES = 56 * 1024 * 1024
WIDEST_BYTES = 62 * 1024 * 1024
SEND_BYTES = 50 * 1024 * 1024


def sector_mask(left_sizes, right_sizes, block_size):
    positions = jnp.arange(block_size, dtype=jnp.int32)
    row_ok = positions[None, :, None] < left_sizes[:, None, None]
    col_ok = positions[None, None, :] < right_sizes[:, None, None]
    return (row_ok & col_ok).astype(jnp.float32)


def pack_blocks(outgoing, targets, term_ids, sector_local, capacity, slot_count):
    target_device = targets // sector_local
    target_place = targets % sector_local
    count_out = targets.shape[0]
    order_index = jnp.arange(count_out, dtype=jnp.int32)
    same_device = target_device[:, None] == target_device[None, :]
    earlier = order_index[None, :] < order_index[:, None]
    peer_rank = jnp.sum((same_device & earlier).astype(jnp.int32), axis=1)
    send_slot = target_device * capacity + peer_rank
    chosen = jnp.arange(slot_count, dtype=jnp.int32)[:, None] == send_slot[None, :]
    slot_source = jnp.sum(jnp.where(chosen, order_index[None, :], 0), axis=1)
    filled = jnp.any(chosen, axis=1)
    buffer = jnp.where(filled[:, None, None], outgoing[slot_source], 0.0)
    left_code = term_ids * sector_local + target_place
    meta_codes = jnp.where(filled, left_code[slot_source], -1)
    return (buffer, meta_codes)


def apply_left(received, meta_codes, flat_left, sector_local, live_count):
    slot_count = meta_codes.shape[0]
    is_valid = meta_codes >= 0
    live_rank = jnp.cumsum(is_valid.astype(jnp.int32)) - 1
    wanted = jnp.arange(live_count, dtype=jnp.int32)
    picked = (live_rank[None, :] == wanted[:, None]) & is_valid[None, :]
    slot_index = jnp.arange(slot_count, dtype=jnp.int32)
    source_slot = jnp.sum(jnp.where(picked, slot_index[None, :], 0), axis=1)
    compact_blocks = received[source_slot]
    compact_codes = meta_codes[source_slot]
    chosen_left = flat_left[compact_codes]
    landed = jnp.einsum(
        "pab,pbc->pac", chosen_left, compact_blocks, precision=lax.Precision.HIGHEST
    )
    target_place = compact_codes % sector_local
    onehot_place = target_place[:, None] == jnp.arange(sector_local, dtype=jnp.int32)[None, :]
    return jnp.einsum(
        "pk,pac->kac", onehot_place.astype(jnp.float32), landed, precision=lax.Precision.HIGHEST
    )


def dense_program(psi_blocks, left_env, right_env, left_sizes, right_sizes, dest_sector):
    term_local = left_env.shape[0]
    sector_local = left_env.shape[1]
    block_size = left_env.shape[2]
    peers = lax.axis_size("sec")
    capacity = (term_local * sector_local + peers - 1) // peers
    slot_count = peers * capacity
    valid_mask = sector_mask(left_sizes, right_sizes, block_size)
    masked_psi = psi_blocks * valid_mask
    carried = jnp.einsum("sab,tsbc->tsac", masked_psi, right_env, precision=lax.Precision.HIGHEST)
    flat_left = left_env.reshape(term_local * sector_local, block_size, block_size)
    term_ids = jnp.repeat(jnp.arange(term_local, dtype=jnp.int32), sector_local)
    buffer, meta_codes = pack_blocks(
        carried.reshape(term_local * sector_local, block_size, block_size),
        dest_sector.reshape(term_local * sector_local),
        term_ids,
        sector_local,
        capacity,
        slot_count,
    )
    received, codes_in = (
        lax.all_to_all(buffer, "sec", split_axis=0, concat_axis=0, tiled=True),
        lax.all_to_all(meta_codes, "sec", split_axis=0, concat_axis=0, tiled=True),
    )
    partial_sum = apply_left(received, codes_in, flat_left, sector_local, term_local * sector_local)
    total = lax.psum(partial_sum, "term")
    return total * valid_mask


def split3(a):
    hi = a.astype(jnp.bfloat16)
    lo = (a - hi.astype(jnp.float32)).astype(jnp.bfloat16)
    return hi, lo


def dot3(a, b, transposed=False):
    dims = (((1,), (1 if transposed else 0,)), ((), ()))
    mul = functools.partial(
        lax.dot_general, dimension_numbers=dims, preferred_element_type=jnp.float32
    )
    return mul(a[0], b[0]) + (mul(a[0], b[1]) + mul(a[1], b[0]))


T_START, T_ROWS, T_NX, T_NY, T_LEFT, T_RIGHT, T_BASE = 0, 1, 2, 3, 4, 5, 6
T_WIDTH = 10


def tile_rows(stream, rows):
    return (stream & 3) * (ROWS * rows) + jnp.minimum(stream >> 2, rows - 1)


def tile_at(a):
    return pl.ds(pl.multiple_of(a * ROWS, ROWS), ROWS)


def strip_at(strip):
    return pl.ds(strip * LANES, LANES)


def block_at(i):
    return pl.ds(pl.multiple_of(i * LANES, LANES), LANES)


def variants(m_blocks, k_blocks, n_blocks, body):
    code = m_blocks * 4 + k_blocks * 2 + n_blocks - 7
    for m in (1, 2):
        for k in (1, 2):
            for n in (1, 2):
                @pl.when((code == m * 4 + k * 2 + n - 7) & (k_blocks > 0))
                def _():
                    body(m * LANES, k * LANES, n * LANES)


S_PSI, S_PROD, S_TURN, S_RIGHT, STRIPS = 0, 2, 6, 10, 14
TOGETHER = 2


def carry_kernel(left_sizes, right_sizes, psi_ref, right_ref, strip_ref):
    row = lax.broadcasted_iota(jnp.int32, (BLK, BLK), 0)
    col = lax.broadcasted_iota(jnp.int32, (BLK, BLK), 1)

    def put(i, first, block):
        for strip in range(2):
            strip_ref[i, first + strip] = block[:, strip * LANES : (strip + 1) * LANES]

    for i in range(TOGETHER):
        d = pl.program_id(0) * TOGETHER + i
        kept = (row < left_sizes[d]) & (col < right_sizes[d])
        psi = jnp.where(kept, psi_ref[i], 0.0)
        parts = split3(psi)
        put(i, S_PSI, psi.T)
        for t in range(PAIRS // HELD):
            right = right_ref[t, i]
            product = dot3(parts, split3(right))
            put(i, S_RIGHT + 2 * t, right)
            put(i, S_PROD + 2 * t, product)
            put(i, S_TURN + 2 * t, product.T)


def send_kernel(slot, source, rows, first, strip_ref, buf_ref, held_ref, sems):
    def copy(p, c):
        e = 4 * p + c
        return pltpu.make_async_copy(strip_ref.at[source[p, c]], held_ref.at[e], sems.at[e])

    places = [(p, c) for p in range(PAIRS) for c in range(4)]
    for p, c in places:
        @pl.when(rows[p, c] > 0)
        def _():
            copy(p, c).start()

    for p, c in places:
        @pl.when(rows[p, c] > 0)
        def _():
            copy(p, c).wait()
            begin = first[p, c]

            def four(i, inner):
                for k in range(4):
                    a = i * 4 + k
                    at = tile_rows(begin + a, slot)
                    tile = held_ref[4 * p + c, tile_at(a), :]
                    buf_ref[pl.ds(at, ROWS, stride=slot), :] = tile
                return inner

            lax.fori_loop(0, (rows[p, c] + 3) >> 2, four, 0)


def relay_kernel(slot, idx, count, in_ref, out_ref):
    def fill(peer, carry):
        def some(i, inner):
            at = peer * slot + i * ROWS
            for k in range(ROWS):
                out_ref[pl.ds(at + k, 1), :] = in_ref[pl.ds(idx[at + k], 1), :]
            return inner

        lax.fori_loop(0, (count[peer] + ROWS - 1) >> 3, some, 0)
        return carry

    lax.fori_loop(0, PEERS, fill, 0)


STREAM = MEMBERS * PIECE
SENT = PIECE + 1


def piece_at(place, core, chip):
    piece = ((place >> 2) ^ core) * 4 + ((place & 3) ^ chip)
    return pl.ds(pl.multiple_of(piece * PIECE, PIECE), PIECE)


def land_kernel(
    slot, tbl, out_tbl, buf_ref, left_ref, keep_ref, send_ref, x_ref, y_ref, z_ref, sum_ref, stream_ref
):
    z_ref[...] = jnp.zeros_like(z_ref)

    def take(dst_ref, u, strip, before, rows):
        at = u * T_WIDTH
        start = tbl[at + T_START] + before
        begin = []
        for k in range(4):
            kind = (start + k) & 3
            rank = tbl[at + T_BASE + kind] + ((before + k) >> 2)
            begin.append((kind * (ROWS * slot), rank))

        def four(i, carry):
            for k in range(4):
                first, rank = begin[k]
                row = first + jnp.minimum(rank + i, slot - 1)
                dst_ref[u, tile_at(i * 4 + k), strip_at(strip)] = buf_ref[
                    pl.ds(row, ROWS, stride=slot), :
                ]
            return carry

        lax.fori_loop(0, (rows + 3) >> 2, four, 0)

    def unpack(u, carry):
        at = u * T_WIDTH
        rows, nx, ny = tbl[at + T_ROWS], tbl[at + T_NX], tbl[at + T_NY]
        for strip in range(2):
            @pl.when(strip < nx)
            def _():
                take(x_ref, u, strip, strip * rows, rows)

            @pl.when(strip < ny)
            def _():
                take(y_ref, u, strip, (nx + strip) * rows, rows)

        return carry

    lax.fori_loop(0, PAIRS, unpack, 0)

    def blocks(rows):
        return (rows * ROWS + LANES - 1) >> 7

    def sector(d, carry):
        first, out_rows, strips, flip, m_blocks, n_blocks = (out_tbl[6 * d + i] for i in range(6))
        units = [d + t * HELD for t in range(PAIRS // HELD)]
        rows = [tbl[u * T_WIDTH + T_ROWS] for u in units]
        nx = [tbl[u * T_WIDTH + T_NX] for u in units]
        ny = [tbl[u * T_WIDTH + T_NY] for u in units]

        def masked(ref, t, height, width, count):
            row = lax.broadcasted_iota(jnp.int32, (height, width), 0)
            col = lax.broadcasted_iota(jnp.int32, (height, width), 1)
            kept = (row < rows[t] * ROWS) & (col < count * LANES)
            return jnp.where(kept, ref[units[t], :height, :width], 0.0)

        def turned(m, k, n):
            for t in range(2):
                z_ref[t, :m, :n] = dot3(
                    split3(left_ref[units[t], :m, :k]),
                    split3(masked(x_ref, t, n, k, nx[t])),
                    transposed=True,
                )

        inner_x = [jnp.where(nx[t] > 0, blocks(rows[t]), 0) for t in range(2)]
        variants(
            m_blocks, jnp.maximum(nx[0], nx[1]), jnp.maximum(inner_x[0], inner_x[1]), turned
        )

        def added(m, k, n):
            total = None
            for t in range(2):
                a = jnp.where(nx[t] > 0, z_ref[t, :m, :k], left_ref[units[t], :m, :k])
                part = dot3(split3(a), split3(masked(y_ref, t, k, n, ny[t])))
                part = part + jnp.where(ny[t] > 0, 0.0, z_ref[t, :m, :n])
                total = part if total is None else total + part

            @pl.when(flip == 0)
            def _():
                sum_ref[:m, :n] = total

            @pl.when(flip != 0)
            def _():
                sum_ref[:n, :m] = total.T

        inner_y = [jnp.where(ny[t] > 0, blocks(rows[t]), 1) for t in range(2)]
        variants(m_blocks, jnp.maximum(inner_y[0], inner_y[1]), n_blocks, added)

        for strip in range(2):
            @pl.when(strip < strips)
            def _():
                begin = first + strip * out_rows

                def four(i, inner):
                    at = jnp.minimum(begin + i * 4, STREAM)
                    for k in range(4):
                        stream_ref[at + k] = sum_ref[tile_at(i * 4 + k), strip_at(strip)]
                    return inner

                lax.fori_loop(0, (out_rows + 3) >> 2, four, 0)
        return carry

    lax.fori_loop(0, HELD, sector, 0)
    core, chip = out_tbl[O_CORE], out_tbl[O_CHIP]
    flag = jnp.full((ROWS, LANES), out_tbl[O_FLAG], jnp.int32).astype(jnp.float32)
    for place in range(4):
        into = pl.ds(place * SENT, PIECE)
        keep_ref[into] = stream_ref[piece_at(place, core, chip)]
        send_ref[into] = stream_ref[piece_at(place + 4, core, chip)]
        keep_ref[place * SENT + PIECE] = flag
        send_ref[place * SENT + PIECE] = flag


def spread_kernel(
    out_tbl, left_sizes, right_sizes, own_ref, other_ref, out_ref, stream_ref, block_ref, sems
):
    core, chip = out_tbl[O_CORE], out_tbl[O_CHIP]
    for place in range(4):
        part = pl.ds(place * SENT, PIECE)
        stream_ref[piece_at(place, core, chip)] = own_ref[part]
        stream_ref[piece_at(place + 4, core, chip)] = other_ref[part]

    row = lax.broadcasted_iota(jnp.int32, (ROWS, LANES), 0)
    col = lax.broadcasted_iota(jnp.int32, (ROWS, LANES), 1)
    def copy(d):
        return pltpu.make_async_copy(block_ref.at[d], out_ref.at[d], sems.at[d])

    def sector(d, carry):
        first, rows, strips, flip, high, wide = (out_tbl[6 * d + i] for i in range(6))
        height = jnp.where(flip > 0, right_sizes[d], left_sizes[d])
        width = jnp.where(flip > 0, left_sizes[d], right_sizes[d])
        block_ref[d] = jnp.zeros((BLK, BLK), jnp.float32)
        for strip in range(2):
            @pl.when(strip < strips)
            def _():
                begin = first + strip * rows
                col_ok = col + strip * LANES < width

                def four(i, inner):
                    at = jnp.minimum(begin + i * 4, STREAM)
                    for k in range(4):
                        a = i * 4 + k
                        kept = col_ok & (row + a * ROWS < height)
                        tile = jnp.where(kept, stream_ref[at + k], 0.0)
                        block_ref[d, tile_at(a), strip_at(strip)] = tile
                    return inner

                lax.fori_loop(0, (rows + 3) >> 2, four, 0)

        for n in (1, 2):
            for m in (1, 2):
                @pl.when((flip > 0) & (wide == n) & (high == m))
                def _():
                    rows, cols = n * LANES, m * LANES
                    turned = block_ref[d, :rows, :cols].T
                    if m < n:
                        block_ref[d, cols:rows, :cols] = jnp.zeros((rows - cols, cols), jnp.float32)
                    if n < m:
                        block_ref[d, :rows, rows:cols] = jnp.zeros((rows, cols - rows), jnp.float32)
                    block_ref[d, :cols, :rows] = turned

        copy(d).start()
        return carry

    def finish(d, carry):
        copy(d).wait()
        return carry

    lax.fori_loop(0, HELD, sector, 0)
    lax.fori_loop(0, HELD, finish, 0)


O_CORE, O_CHIP, O_FLAG = 6 * HELD, 6 * HELD + 1, 6 * HELD + 2

SMEM = pl.BlockSpec(memory_space=pltpu.SMEM)
VMEM = pl.BlockSpec(memory_space=pltpu.VMEM)
PARAMS = pltpu.CompilerParams(vmem_limit_bytes=VMEM_BYTES)
WIDEST = pltpu.CompilerParams(vmem_limit_bytes=WIDEST_BYTES)
WIDE = pltpu.CompilerParams(vmem_limit_bytes=WIDE_BYTES)


def floats(*shape):
    return jax.ShapeDtypeStruct(shape, jnp.float32)


def scratch(*shape):
    return pltpu.VMEM(shape, jnp.float32)


def carry_call(left_sizes, right_sizes, psi, right):
    return pl.pallas_call(
        carry_kernel,
        grid=(HELD // TOGETHER,),
        out_shape=floats(HELD, STRIPS, BLK, LANES),
        in_specs=[
            SMEM,
            SMEM,
            pl.BlockSpec((TOGETHER, BLK, BLK), lambda d: (d, 0, 0)),
            pl.BlockSpec((PAIRS // HELD, TOGETHER, BLK, BLK), lambda d: (0, d, 0, 0)),
        ],
        out_specs=pl.BlockSpec((TOGETHER, STRIPS, BLK, LANES), lambda d: (d, 0, 0, 0)),
        cost_estimate=pl.CostEstimate(
            flops=6 * PAIRS * BLK**3, bytes_accessed=24 * 2**20, transcendentals=0
        ),
        compiler_params=WIDE,
    )(left_sizes, right_sizes, psi, right)


def send_call(slot, tables, strips):
    return pl.pallas_call(
        functools.partial(send_kernel, slot),
        out_shape=floats(PEERS * slot, LANES),
        in_specs=[SMEM, SMEM, SMEM, pl.BlockSpec(memory_space=pl.ANY)],
        out_specs=VMEM,
        scratch_shapes=[
            scratch(4 * PAIRS, BLK, LANES),
            pltpu.SemaphoreType.DMA((4 * PAIRS,)),
        ],
        compiler_params=pltpu.CompilerParams(vmem_limit_bytes=SEND_BYTES),
    )(*tables, strips)


def relay_call(slot, idx, count, received):
    return pl.pallas_call(
        functools.partial(relay_kernel, slot),
        out_shape=floats(PEERS * slot, LANES),
        in_specs=[SMEM, SMEM, VMEM],
        out_specs=VMEM,
        compiler_params=PARAMS,
    )(idx, count, received)


def land_call(slot, tbl, out_tbl, received, left):
    return pl.pallas_call(
        functools.partial(land_kernel, slot),
        out_shape=[floats(4 * SENT, ROWS, LANES)] * 2,
        in_specs=[SMEM, SMEM, VMEM, VMEM],
        out_specs=[VMEM, VMEM],
        scratch_shapes=[
            scratch(PAIRS, BLK, BLK),
            scratch(PAIRS, BLK, BLK),
            scratch(PAIRS // HELD, BLK, BLK),
            scratch(BLK, BLK),
            scratch(STREAM + ROWS, ROWS, LANES),
        ],
        compiler_params=PARAMS,
    )(tbl, out_tbl, received, left)


def spread_call(out_tbl, left_sizes, right_sizes, own, other):
    return pl.pallas_call(
        spread_kernel,
        out_shape=floats(HELD, BLK, BLK),
        in_specs=[SMEM, SMEM, SMEM, VMEM, VMEM],
        out_specs=pl.BlockSpec(memory_space=pl.ANY),
        scratch_shapes=[
            scratch(STREAM + ROWS, ROWS, LANES),
            scratch(HELD, BLK, BLK),
            pltpu.SemaphoreType.DMA((HELD,)),
        ],
        compiler_params=WIDEST,
    )(out_tbl, left_sizes, right_sizes, own, other)


def up(value, unit):
    return (value + (unit - 1)) >> (unit.bit_length() - 1)


def before(values, axis):
    n = values.shape[axis]
    moved = jnp.moveaxis(values, axis, -1)
    lower = np.arange(n)[:, None] > np.arange(n)[None, :]
    total = jnp.sum(jnp.where(lower, moved[..., None, :], 0), axis=-1)
    return jnp.moveaxis(total, -1, axis)


def make_tables(facts, me, core, chip):
    size_l, size_r = facts[:, 0], facts[:, 1]
    dest = facts[:, 2:].reshape(PEERS, PAIRS)

    ls = jnp.concatenate([size_l, size_l], axis=1)
    rs = jnp.concatenate([size_r, size_r], axis=1)
    to_dev = dest >> 3
    hit_dev = to_dev[:, :, None] == np.arange(PEERS, dtype=np.int32)[None, None, :]
    sector = np.arange(PEERS * HELD, dtype=np.int32)[:, None]
    rd = jnp.sum(
        jnp.where(dest.reshape(1, -1) == sector, size_r.reshape(-1)[:, None], 0), axis=0
    ).reshape(PEERS, PAIRS)
    nl, nr = up(ls, LANES), up(rd, LANES)
    cost_c = up(ls, ROWS) * nr
    cost_ct = up(rd, ROWS) * nl
    cost_f = up(rs, ROWS) * (nl + nr)
    is_f = (cost_f < cost_c) & (cost_f < cost_ct)
    is_ct = ~is_f & (cost_ct < cost_c)
    rows = up(jnp.where(is_f, rs, jnp.where(is_ct, rd, ls)), ROWS)
    nx = jnp.where(is_f | is_ct, nl, 0)
    ny = jnp.where(is_ct, 0, nr)
    tiles = rows * (nx + ny)
    start = before(tiles, 1)
    total = jnp.sum(tiles, axis=1)

    kinds = np.arange(4, dtype=np.int32)[:, None, None]
    lag = (kinds - start) & 3
    share = (tiles + 3 - lag) >> 2
    first_row = (start + lag) >> 2
    onto = jnp.sum(jnp.where(hit_dev[None], share[..., None], 0), axis=2)
    base = before(onto, 1)
    filled = jnp.sum(onto, axis=1)

    high, wide = up(size_l, LANES), up(size_r, LANES)
    flip = (up(size_r, ROWS) * high < up(size_l, ROWS) * wide).astype(jnp.int32)
    out_rows = up(jnp.where(flip > 0, size_r, size_l), ROWS)
    out_strips = jnp.where(flip > 0, high, wide)
    out_tiles = out_rows * out_strips
    out_first = before(out_tiles, 1)
    crowded = jnp.any(jnp.sum(out_tiles, axis=1) > MEMBERS * PIECE)

    def spilled(slot):
        return jnp.any(total > 4 * (slot - 1)) | jnp.any(filled > slot) | crowded

    def own(values, axis=0):
        return lax.dynamic_index_in_dim(values, me, axis, keepdims=False)

    pair = np.arange(PAIRS, dtype=np.int32)[:, None]
    place = np.arange(4, dtype=np.int32)[None, :]
    own_nx, own_ny, own_rows = own(nx)[:, None], own(ny)[:, None], own(rows)[:, None]
    both = (own_nx > 0) & (own_ny > 0)
    term, held = pair // HELD, pair % HELD
    source = jnp.where(
        place < 2,
        jnp.where(both, S_PSI, S_TURN + 2 * term),
        jnp.where(both, S_RIGHT, S_PROD) + 2 * term,
    )
    source = held * STRIPS + source + place % 2
    used = jnp.where(place < 2, place < own_nx, place - 2 < own_ny)
    index = jnp.where(place < 2, place, own_nx + place - 2)
    send_tbl = (
        source,
        jnp.where(used, own_rows, 0),
        own(start)[:, None] + index * own_rows,
    )

    kind = me >> 3
    onto_k = lax.dynamic_index_in_dim(onto, kind, 0, keepdims=False)
    base_k = lax.dynamic_index_in_dim(base, kind, 0, keepdims=False)
    first_k = lax.dynamic_index_in_dim(first_row, kind, 0, keepdims=False)
    filled_k = lax.dynamic_index_in_dim(filled, kind, 0, keepdims=False)
    first_to = jnp.sum(jnp.where(hit_dev, first_k[:, :, None], 0), axis=1)

    def relay_tbl(slot):
        rank = np.arange(slot, dtype=np.int32)[None, None, :]
        here = (rank >= base_k[:, :, None]) & (rank < (base_k + onto_k)[:, :, None])
        origin = np.arange(PEERS, dtype=np.int32)[:, None] * slot + first_to - base_k
        idx = jnp.sum(jnp.where(here, origin[:, :, None] + rank, 0), axis=0)
        return jnp.clip(idx, 0, PEERS * slot - 1).reshape(-1), jnp.minimum(filled_k, slot)

    unit = np.arange(PAIRS, dtype=np.int32)[:, None, None]
    reach = (dest[None] == me * HELD + unit % HELD) & (
        (np.arange(PAIRS, dtype=np.int32) // HELD)[None, None, :] == unit // HELD
    )

    def reached(values):
        return jnp.sum(jnp.where(reach, values[None], 0), axis=(1, 2))

    base_me = lax.dynamic_index_in_dim(base, me, 2, keepdims=False)
    land_tbl = jnp.stack(
        [reached(start), reached(rows), reached(nx), reached(ny), reached(ls), reached(rs)]
        + [reached(jnp.broadcast_to(base_me[g][:, None], (PEERS, PAIRS))) for g in range(4)],
        axis=1,
    ).reshape(-1)

    def out_tbl(slot):
        lines = [own(v) for v in (out_first, out_rows, out_strips, flip, high, wide)]
        last = jnp.stack([core, chip, spilled(slot).astype(jnp.int32)]).astype(jnp.int32)
        return jnp.concatenate([jnp.stack(lines, axis=1).reshape(-1), last])

    return send_tbl, relay_tbl, land_tbl, out_tbl


def per_device(psi_blocks, left_env, right_env, left_sizes, right_sizes, dest_sector):
    me = lax.axis_index("sec")
    member = lax.axis_index("term")
    core, chip = member & 1, member >> 1
    strips = carry_call(left_sizes, right_sizes, psi_blocks, right_env)
    strips = strips.reshape(HELD * STRIPS, BLK, LANES)
    facts = [left_sizes[None], right_sizes[None], dest_sector]
    mine = jnp.concatenate(
        [jnp.broadcast_to(v[None], (PEERS,) + v.shape) for v in facts], axis=1
    )
    facts = lax.all_to_all(mine, "sec", 0, 0, tiled=True)
    tables = make_tables(facts, me, core, chip)
    send_tbl, relay_tbl, land_tbl, out_tbl = tables

    def swap(values, bits):
        return lax.ppermute(values, "term", [(i, i ^ bits) for i in range(MEMBERS)])

    def packed_program(slot, otherwise):
        def exchange(rows):
            there = lax.all_to_all(rows.reshape(PEERS, slot, LANES), "sec", 0, 0, tiled=True)
            return there.reshape(PEERS * slot, LANES)

        arrived = exchange(send_call(slot, send_tbl, strips))
        idx, count = relay_tbl(slot)
        arrived = exchange(relay_call(slot, idx, count, arrived))
        left = left_env.reshape(PAIRS, BLK, BLK)
        lines = out_tbl(slot)
        keep, give = land_call(slot, land_tbl, lines, arrived, left)
        half = (keep + swap(give, 1)).reshape(4, SENT, ROWS, LANES)
        piece = half[0] + swap(half[1], 2) + swap(half[2], 4) + swap(half[3], 6)
        whole = jnp.concatenate([piece, swap(piece, 2), swap(piece, 4), swap(piece, 6)])
        other = swap(whole, 1)
        return lax.cond(
            piece[PIECE, 0, 0] > 0.5,
            otherwise,
            lambda: spread_call(lines, left_sizes, right_sizes, whole, other),
        )

    def dense():
        return dense_program(
            psi_blocks, left_env, right_env, left_sizes, right_sizes, dest_sector
        )

    usual, tall = SLOT_ROWS
    return packed_program(usual, lambda: packed_program(tall, dense))


def solution(mesh):
    in_specs = (
        P("sec", None, None),
        P("term", "sec", None, None),
        P("term", "sec", None, None),
        P("sec"),
        P("sec"),
        P("term", "sec"),
    )
    out_specs = P("sec", None, None)
    return jax.shard_map(
        per_device, mesh=mesh, in_specs=in_specs, out_specs=out_specs, check_vma=False
    )
```
